32 devices in a mesh: grp: 2 (over y), gx: 4 (over z), gy: 4 (over x, core).
Axes of the slice: x: 2, y: 2, z: 4, core: 2. Of those that a mesh axis runs over, the one named last changes fastest.
Arguments:
- source: bfloat16 [512, 256, 128], P(('grp', 'gx'), 'gy'), parts along dimension 0, may hold values from -6 to 6
- field: bfloat16 [512, 256, 128], P(('grp', 'gx'), 'gy'), parts along dimension 0, may hold values from -3 to 3
- kerr: float32 [512, 256], P(('grp', 'gx'), 'gy'), parts along dimension 0, may hold values from 0.05 to 0.3
- wave: float32 [512, 256], P(('grp', 'gx'), 'gy'), parts along dimension 0, may hold values from 0.5 to 2
- leaf_ops: bfloat16 [16, 16, 256, 256], P('gx', 'gy'), may hold values from -0.375 to 0.375
- transfer_ops: float32 [4, 256, 64], P('gx', 'gy'), may hold values from 0 to 1
Outputs:
- updated: bfloat16 [512, 256, 128], P(('grp', 'gx'), 'gy'), parts along dimension 0
- residual: bfloat16 [512, 256, 128], P(('grp', 'gx'), 'gy'), parts along dimension 0
The draws below stay inside these ranges and needn't reach their ends.
There are 2 independent parts, one for each index of `grp`. The reference program is written for one: setup_inputs(seed, part) draws one part's arguments, and reference() takes and returns one part's arrays. A program takes and returns all parts, laid end to end along the dimension named above; an argument that names none is the same for every part. Nothing has to cross between parts.
All inputs are finite; a program needn't handle non-finite values.
Results may differ from the reference program's by a relative error of at most 0.015.
Values may be sent and summed in bfloat16 or wider, within the bound.
A program may use at most 64 MiB of HBM per device.

```python
import math
import jax
import jax.numpy as jnp
from jax import lax

Q = 16
P_SIZE = 256
LX = 4
LY = 4
B = 128
XD = 64
YD = 64
NXP = 256
NYP = 256
N_GX = 4
N_GY = 4


def draw_transfer_ops(key, part):
    random_key_list = jax.random.split(key, 6)
    row_count = N_GY * YD
    growth_rates = jnp.exp(jax.random.uniform(random_key_list[0], (row_count,), jnp.float32, math.log(0.5 / N_GX), math.log(2.0)))
    spread_width = jax.random.uniform(random_key_list[1], (N_GX, 1, 1), jnp.float32, 0.5, 1.5)
    pulse_trains = jnp.where(jax.random.uniform(random_key_list[2], (N_GX, 1, 1), jnp.float32) < 3.0 / N_GX, 0.6, 1.0)
    damping_factor = jnp.exp(-growth_rates[None, :, None] * spread_width) * pulse_trains
    row_pos = (jnp.arange(row_count) % YD)[:, None].astype(jnp.float32)
    col_pos = jnp.arange(YD)[None, :].astype(jnp.float32)
    distance = jnp.abs(row_pos - col_pos)
    on_diagonal = distance < 0.5
    rough_factor = jax.random.uniform(random_key_list[3], (N_GX, row_count, YD), jnp.float32, 0.5, 1.0)
    kernel_width = jax.random.uniform(random_key_list[4], (N_GX, row_count, 1), jnp.float32, 2.0, 8.0)
    off_entries = jnp.where(on_diagonal[None], 0.0, rough_factor * jnp.exp(-distance[None] / kernel_width))
    off_total = jnp.sum(off_entries, axis=2, keepdims=True)
    keep_share = jax.random.uniform(random_key_list[5], (N_GX, row_count, 1), jnp.float32, 0.6, 0.75)
    mixed_map = jnp.where(on_diagonal[None], keep_share, (1.0 - keep_share) * off_entries / off_total)
    return damping_factor * mixed_map


def block_scale(rng, extent, cuts, low, largest):
    factor_of, own = 1.0, jax.random.fold_in(rng, 6)
    for dim, shards_of in cuts:
        draws = jnp.exp(jax.random.uniform(jax.random.fold_in(own, dim), (shards_of,), jnp.float32, low / len(cuts), largest / len(cuts)))
        factor_of = factor_of * jnp.repeat(draws, extent[dim] // shards_of).reshape([-1 if axis == dim else 1 for axis in range(len(extent))])
    return factor_of


def scatter_about(own_key, extent, spread, reach, pieces=(), kind=jnp.bfloat16):
    gain = block_scale(own_key, extent, pieces, -0.22, 0.18) if pieces else 1.0
    values = jax.random.normal(own_key, extent, jnp.float32) * spread * gain
    return jnp.minimum(jnp.maximum(values, -reach), reach).astype(kind)


def setup_inputs(seed: int = 0, part: int = 0) -> dict:
    key_of = jax.random.split(jax.random.key(seed), 7)
    part_splits = jax.random.split(jax.random.fold_in(key_of[6], part), 7)
    source = scatter_about(part_splits[0], (NXP, NYP, B), 1.0, 6.0, ((0, 4), (1, 4)))
    field = scatter_about(part_splits[1], (NXP, NYP, B), 0.7, 3.0, ((0, 4), (1, 4)))
    kerr = jnp.clip(jnp.exp(math.log(0.3) - 1.7917595 * jax.random.uniform(part_splits[2], (NXP, NYP), jnp.float32) ** block_scale(part_splits[2], (NXP, NYP), ((0, 4), (1, 4)), -0.2, 0.2)), 0.05, 0.3)
    wave = jnp.clip(0.5 + 1.5 * jax.random.uniform(part_splits[3], (NXP, NYP), jnp.float32) ** block_scale(part_splits[3], (NXP, NYP), ((0, 4), (1, 4)), -0.2, 0.2), 0.5, 2.0)
    leaf_ops = scatter_about(key_of[4], (N_GX * LX, N_GY * LY, P_SIZE, P_SIZE), P_SIZE ** -0.5, 0.375, ((0, 4), (1, 4)))
    transfer_ops = draw_transfer_ops(jax.random.fold_in(key_of[6], 71), part)
    return dict(source=source, field=field, kerr=kerr, wave=wave, leaf_ops=leaf_ops, transfer_ops=transfer_ops)


lift_weight = 0.3


def reference(source, field, kerr, wave, leaf_ops, transfer_ops):
    source_f = source.astype(jnp.float32)
    field_f = field.astype(jnp.float32)
    kerr_source = (source_f - kerr[:, :, None] * field_f * field_f * field_f).astype(jnp.bfloat16)
    leaves = kerr_source.reshape(N_GX * LX, Q, N_GY * LY, Q, B).transpose(0, 2, 1, 3, 4).reshape(N_GX * LX, N_GY * LY, P_SIZE, B)

    def solve_row(pair):
        return jnp.einsum("bpq,bqn->bpn", pair[0].astype(jnp.float32), pair[1].astype(jnp.float32), precision=lax.Precision.HIGHEST)

    solved = lax.map(solve_row, (leaf_ops, leaves))
    particular_solution = solved.reshape(N_GX * LX, N_GY * LY, Q, Q, B).transpose(0, 2, 1, 3, 4).reshape(NXP, NYP, B)
    slabs = particular_solution.reshape(N_GX, XD, N_GY, YD, B)
    right_face = slabs[:, -1]
    left_face = slabs[:, 0]
    operators = transfer_ops.reshape(N_GX, N_GY, YD, YD)

    def step_up(state, inputs):
        oper_d, face_d = inputs
        nxt = jnp.einsum("gij,gjb->gib", oper_d, state, precision=lax.Precision.HIGHEST) + face_d
        return nxt, state

    def step_down(state, inputs):
        oper_d, face_d = inputs
        nxt = jnp.einsum("gji,gjb->gib", oper_d, state, precision=lax.Precision.HIGHEST) + face_d
        return nxt, state

    start = jnp.zeros((N_GY, YD, B), jnp.float32)
    _, w_in = lax.scan(step_up, start, (operators, right_face))
    _, z_in = lax.scan(step_down, start, (operators, left_face), reverse=True)
    position = jnp.arange(XD).astype(jnp.float32)
    left_prof = ((XD - position) / XD)[None, :, None, None, None]
    right_prof = ((position + 1.0) / XD)[None, :, None, None, None]
    lifted = slabs + lift_weight * (left_prof * w_in[:, None] + right_prof * z_in[:, None])
    updated = lifted.reshape(NXP, NYP, B).astype(jnp.bfloat16)
    values = updated.astype(jnp.float32)
    padded_patches = jnp.pad(values, ((1, 1), (1, 1), (0, 0)))
    laplacian_operator = padded_patches[2:, 1:-1] + padded_patches[:-2, 1:-1] + padded_patches[1:-1, 2:] + padded_patches[1:-1, :-2] - 4.0 * values
    residual = laplacian_operator + wave[:, :, None] * values + kerr[:, :, None] * values * values * values - source_f
    return updated, residual.astype(jnp.bfloat16)
```

```python
import functools

import jax
import jax.numpy as jnp
from jax import lax
from jax.experimental import pallas as pl
from jax.experimental.pallas import tpu as pltpu
from jax.sharding import PartitionSpec as P

lift_weight = 0.3
MESH = pl.DeviceIdType.MESH
F32 = jnp.float32
BF16 = jnp.bfloat16
PAD = 8


def kernel(
    n_gx, n_gy,
    source, field, kerr, wave, leaf_ops, transfer_ops,
    updated, residual,
    src_v, fld_v, kerr_v, wave_v, map_v, ops_v, edge_ops, leaf_src, grid, kerr_b, wave_b,
    upd_v, res_v, face_out, face_in, op_out, op_in, edge_out, edge_in,
    row_sems, small_sems, ops_sems, edge_sems, out_sems,
    face_send, face_recv, op_send, op_recv, halo_send, halo_recv,
):
    x_points, y_points, columns = src_v.shape
    leaves_x, leaves_y, leaf_pts, _ = ops_v.shape
    q = x_points // leaves_x
    half = y_points // 2
    last = leaves_x - 1
    me = lax.axis_index("gx")
    col = lax.axis_index("gy")

    small = [
        pltpu.make_async_copy(kerr, kerr_v, small_sems.at[0]),
        pltpu.make_async_copy(wave, wave_v, small_sems.at[1]),
        pltpu.make_async_copy(transfer_ops.at[0], map_v, small_sems.at[2]),
    ]
    for c in small:
        c.start()
    order = [0, last] + list(range(1, last))
    rows, edges, ops = {}, [], {}
    for a in order:
        span = pl.ds(a * q, q)
        rows[a] = (
            pltpu.make_async_copy(source.at[span], src_v.at[span], row_sems.at[0, a]),
            pltpu.make_async_copy(field.at[span], fld_v.at[span], row_sems.at[1, a]),
        )
    for i, (a, first) in enumerate(((0, 0), (last, leaf_pts - q))):
        edges.append(
            pltpu.make_async_copy(
                leaf_ops.at[a, :, pl.ds(first, q), :], edge_ops.at[i], edge_sems.at[i]
            )
        )
    for a in order:
        ops[a] = pltpu.make_async_copy(leaf_ops.at[a], ops_v.at[a], ops_sems.at[a])
    for a in order[:2]:
        rows[a][0].start()
        rows[a][1].start()
    for c in edges:
        c.start()
    for a in order[2:]:
        rows[a][0].start()
        rows[a][1].start()
    for a in order:
        ops[a].start()

    barrier = pltpu.get_barrier_semaphore()

    def greet(p, carry):
        @pl.when(p != me)
        def _():
            pl.semaphore_signal(barrier, inc=1, device_id={"gx": p}, device_id_type=MESH)

        return carry

    lax.fori_loop(0, n_gx, greet, 0)

    @pl.when(col > 0)
    def _():
        pl.semaphore_signal(barrier, inc=1, device_id={"gy": col - 1}, device_id_type=MESH)

    @pl.when(col < n_gy - 1)
    def _():
        pl.semaphore_signal(barrier, inc=1, device_id={"gy": col + 1}, device_id_type=MESH)

    partners = (n_gx - 1) + jnp.where(col > 0, 1, 0) + jnp.where(col < n_gy - 1, 1, 0)

    for c in small:
        c.wait()
    coeff = jnp.transpose(jnp.concatenate([kerr_v[...], wave_v[...]], axis=0))
    own = map_v[...]
    own_t = jnp.transpose(own)
    for i, m in enumerate((own, own_t)):
        op_out[i] = jnp.concatenate([m[:half], m[half:]], axis=1).astype(BF16)

    def face_copy(side, slot, p):
        return pltpu.make_async_remote_copy(
            src_ref=face_out.at[side],
            dst_ref=face_in.at[slot],
            send_sem=face_send.at[p],
            recv_sem=face_recv.at[slot],
            device_id={"gx": p},
            device_id_type=MESH,
        )

    def op_copy(side, slot, p):
        return pltpu.make_async_remote_copy(
            src_ref=op_out.at[side],
            dst_ref=op_in.at[slot],
            send_sem=op_send.at[p],
            recv_sem=op_recv.at[slot],
            device_id={"gx": p},
            device_id_type=MESH,
        )

    def run(low, high, body):
        def step(p, carry):
            body(p)
            return carry

        lax.fori_loop(low, high, step, 0)

    inner = jnp.logical_and(me > 0, me < n_gx - 1)
    pl.semaphore_wait(barrier, partners)

    @pl.when(inner)
    def _():
        run(me + 1, n_gx, lambda p: op_copy(0, me, p).start())
        run(0, me, lambda p: op_copy(1, me, p).start())

    def leaf_row(a):
        rows[a][0].wait()
        rows[a][1].wait()
        for i in range(q):
            x = a * q + i
            k = jnp.broadcast_to(coeff[:, x : x + 1], (y_points, columns))
            kerr_b[x] = k
            f = fld_v[x].astype(F32)
            s = (src_v[x].astype(F32) - k * f * f * f).astype(BF16)
            for b in range(leaves_y):
                leaf_src[a, b, i * q : (i + 1) * q, :] = s[b * q : (b + 1) * q]

    for i, a in enumerate((0, last)):
        if i == 0 or last > 0:
            leaf_row(a)
        edges[i].wait()
        for b in range(leaves_y):
            face_out[1 - i, b * q : (b + 1) * q, :] = jnp.dot(
                edge_ops[i, b], leaf_src[a, b], preferred_element_type=F32
            ).astype(BF16)
    run(me + 1, n_gx, lambda p: face_copy(0, me, p).start())
    run(0, me, lambda p: face_copy(1, me, p).start())

    for a in order[2:]:
        leaf_row(a)
    for a in order:
        ops[a].wait()
        for b in range(leaves_y):
            solved = jnp.dot(ops_v[a, b], leaf_src[a, b], preferred_element_type=F32)
            for i in range(q):
                grid[1 + a * q + i, PAD + b * q : PAD + (b + 1) * q, :] = solved[i * q : (i + 1) * q]
    for x in range(x_points):
        wave_b[x] = jnp.broadcast_to(
            coeff[:, x_points + x : x_points + x + 1] - 4.0, (y_points, columns)
        )
    zero_row = jnp.zeros((1, columns), F32)
    for x in range(x_points):
        grid[1 + x, PAD - 1 : PAD, :] = zero_row
        grid[1 + x, PAD + y_points : PAD + y_points + 1, :] = zero_row
    low_edge = jnp.concatenate([grid[1 + x, PAD : PAD + 1, :] for x in range(x_points)], axis=0)
    high_edge = jnp.concatenate(
        [grid[1 + x, PAD + y_points - 1 : PAD + y_points, :] for x in range(x_points)], axis=0
    )

    def apply(packed, state):
        s = state.astype(BF16)
        z = jnp.zeros_like(s)
        wide = jnp.concatenate(
            [jnp.concatenate([s, z], axis=1), jnp.concatenate([z, s], axis=1)], axis=0
        )
        out = jnp.dot(packed, wide, preferred_element_type=F32)
        return jnp.concatenate([out[:, :columns], out[:, columns:]], axis=0)

    zeros = jnp.zeros((y_points, columns), F32)

    def arrived(s):
        face_copy(0, s, s).wait_recv()
        return face_in[s].astype(F32)

    def chain(begin, count, step):
        def first():
            return arrived(begin)

        state = lax.cond(count > 0, first, lambda: zeros)

        def hop(i, carry):
            _, now = carry
            s = begin + step * i
            op_copy(0, s, s).wait_recv()
            nxt = apply(op_in[s], now) + arrived(s)
            return now, nxt

        return lax.fori_loop(1, count, hop, (zeros, state))

    w_before, w = chain(0, me, 1)
    z_after, z = chain(n_gx - 1, n_gx - 1 - me, -1)
    w3, z3 = lift_weight * w, lift_weight * z

    position = lax.broadcasted_iota(jnp.int32, (x_points, columns), 0).astype(F32)
    left_prof = (x_points - position) / x_points
    right_prof = (position + 1.0) / x_points
    for i, (edge, y) in enumerate(((low_edge, 0), (high_edge, y_points - 1))):
        edge_out[i] = (
            edge + (left_prof * w3[y : y + 1, :] + right_prof * z3[y : y + 1, :])
        ).astype(BF16)

    def halo_copy(side, p):
        return pltpu.make_async_remote_copy(
            src_ref=edge_out.at[side],
            dst_ref=edge_in.at[1 - side],
            send_sem=halo_send.at[side],
            recv_sem=halo_recv.at[1 - side],
            device_id={"gy": p},
            device_id_type=MESH,
        )

    @pl.when(col > 0)
    def _():
        halo_copy(0, col - 1).start()

    @pl.when(col < n_gy - 1)
    def _():
        halo_copy(1, col + 1).start()

    tip = 1.0 / x_points
    body = pl.ds(PAD, y_points)

    @pl.when(me > 0)
    def _():
        face = face_in[jnp.maximum(me - 1, 0)].astype(F32)
        z_there = apply(op_out[1], z) + grid[1, body, :]
        there = face + lift_weight * (tip * w_before + z_there)
        grid[0, body, :] = there.astype(BF16).astype(F32)

    @pl.when(me == 0)
    def _():
        grid[0, body, :] = zeros

    @pl.when(me < n_gx - 1)
    def _():
        face = face_in[jnp.minimum(me + 1, n_gx - 1)].astype(F32)
        w_there = apply(op_out[0], w) + grid[x_points, body, :]
        there = face + lift_weight * (w_there + tip * z_after)
        grid[x_points + 1, body, :] = there.astype(BF16).astype(F32)

    @pl.when(me == n_gx - 1)
    def _():
        grid[x_points + 1, body, :] = zeros

    outs = []
    for a in range(leaves_x):

        def lift(i, carry):
            x = a * q + i
            at = lax.convert_element_type(x, F32)
            u = grid[1 + x, body, :] + (
                ((x_points - at) / x_points) * w3 + ((at + 1.0) / x_points) * z3
            )
            u = u.astype(BF16)
            upd_v[x] = u
            grid[1 + x, body, :] = u.astype(F32)
            return carry

        lax.fori_loop(0, q, lift, 0, unroll=4)
        span = pl.ds(a * q, q)
        outs.append(pltpu.make_async_copy(upd_v.at[span], updated.at[span], out_sems.at[a]))
        outs[-1].start()

    def finish(x, low, size):
        mid = grid[1 + x, PAD + low : PAD + low + size, :]
        near = (
            grid[x, PAD + low : PAD + low + size, :]
            + grid[2 + x, PAD + low : PAD + low + size, :]
        ) + (
            grid[1 + x, PAD + low - 1 : PAD + low + size - 1, :]
            + grid[1 + x, PAD + low + 1 : PAD + low + size + 1, :]
        )
        factor = wave_b[x, low : low + size, :] + kerr_b[x, low : low + size, :] * (mid * mid)
        res_v[x, low : low + size, :] = (
            near + (factor * mid - src_v[x, low : low + size, :].astype(F32))
        ).astype(BF16)

    def inside(x, carry):
        finish(x, q, y_points - 2 * q)
        return carry

    lax.fori_loop(0, x_points, inside, 0, unroll=4)
    part = pl.ds(q, y_points - 2 * q)
    outs.append(
        pltpu.make_async_copy(
            res_v.at[:, part, :], residual.at[:, part, :], out_sems.at[leaves_x]
        )
    )
    outs[-1].start()

    @pl.when(col > 0)
    def _():
        halo_copy(1, col - 1).wait_recv()
        got = edge_in[0].astype(F32)
        for x in range(x_points):
            grid[1 + x, PAD - 1 : PAD, :] = got[x : x + 1]

    @pl.when(col < n_gy - 1)
    def _():
        halo_copy(0, col + 1).wait_recv()
        got = edge_in[1].astype(F32)
        for x in range(x_points):
            grid[1 + x, PAD + y_points : PAD + y_points + 1, :] = got[x : x + 1]

    def sides(x, carry):
        finish(x, 0, q)
        finish(x, y_points - q, q)
        return carry

    lax.fori_loop(0, x_points, sides, 0, unroll=4)
    for i, low in enumerate((0, y_points - q)):
        part = pl.ds(low, q)
        outs.append(
            pltpu.make_async_copy(
                res_v.at[:, part, :], residual.at[:, part, :], out_sems.at[leaves_x + 1 + i]
            )
        )
        outs[-1].start()

    run(me + 1, n_gx, lambda p: face_copy(0, me, p).wait_send())
    run(0, me, lambda p: face_copy(1, me, p).wait_send())

    @pl.when(inner)
    def _():
        run(me + 1, n_gx, lambda p: op_copy(0, me, p).wait_send())
        run(0, me, lambda p: op_copy(1, me, p).wait_send())

    @pl.when(col > 0)
    def _():
        halo_copy(0, col - 1).wait_send()

    @pl.when(col < n_gy - 1)
    def _():
        halo_copy(1, col + 1).wait_send()

    for c in outs:
        c.wait()


def per_device(n_gx, n_gy, source, field, kerr, wave, leaf_ops, transfer_ops):
    x_points, y_points, columns = source.shape
    leaves_x, leaves_y, leaf_pts, _ = leaf_ops.shape
    q = x_points // leaves_x
    grid_shape = (x_points, y_points, columns)
    dma = pltpu.SemaphoreType.DMA
    anywhere = pl.BlockSpec(memory_space=pl.ANY)
    return pl.pallas_call(
        functools.partial(kernel, n_gx, n_gy),
        out_shape=[jax.ShapeDtypeStruct(grid_shape, BF16)] * 2,
        in_specs=[anywhere] * 6,
        out_specs=[anywhere] * 2,
        scratch_shapes=[
            pltpu.VMEM(grid_shape, BF16),
            pltpu.VMEM(grid_shape, BF16),
            pltpu.VMEM((x_points, y_points), F32),
            pltpu.VMEM((x_points, y_points), F32),
            pltpu.VMEM((y_points, y_points), F32),
            pltpu.VMEM(leaf_ops.shape, BF16),
            pltpu.VMEM((2, leaves_y, q, leaf_pts), BF16),
            pltpu.VMEM((leaves_x, leaves_y, leaf_pts, columns), BF16),
            pltpu.VMEM((x_points + 2, y_points + 2 * PAD, columns), F32),
            pltpu.VMEM(grid_shape, F32),
            pltpu.VMEM(grid_shape, F32),
            pltpu.VMEM(grid_shape, BF16),
            pltpu.VMEM(grid_shape, BF16),
            pltpu.VMEM((2, y_points, columns), BF16),
            pltpu.VMEM((n_gx, y_points, columns), BF16),
            pltpu.VMEM((2, y_points // 2, 2 * y_points), BF16),
            pltpu.VMEM((n_gx, y_points // 2, 2 * y_points), BF16),
            pltpu.VMEM((2, x_points, columns), BF16),
            pltpu.VMEM((2, x_points, columns), BF16),
            dma((2, leaves_x)),
            dma((3,)),
            dma((leaves_x,)),
            dma((2,)),
            dma((leaves_x + 3,)),
            dma((n_gx,)),
            dma((n_gx,)),
            dma((n_gx,)),
            dma((n_gx,)),
            dma((2,)),
            dma((2,)),
        ],
        compiler_params=pltpu.CompilerParams(
            collective_id=0, has_side_effects=True, vmem_limit_bytes=40 * 1024 * 1024
        ),
        cost_estimate=pl.CostEstimate(
            flops=2 * leaf_ops.size * columns, bytes_accessed=6 << 20, transcendentals=0
        ),
        name="kerr_step",
    )(source, field, kerr, wave, leaf_ops, transfer_ops)


def solution(mesh):
    return jax.shard_map(
        functools.partial(per_device, mesh.shape["gx"], mesh.shape["gy"]),
        mesh=mesh,
        in_specs=(
            P(("grp", "gx"), "gy", None),
            P(("grp", "gx"), "gy", None),
            P(("grp", "gx"), "gy"),
            P(("grp", "gx"), "gy"),
            P("gx", "gy", None, None),
            P("gx", "gy", None),
        ),
        out_specs=(P(("grp", "gx"), "gy", None), P(("grp", "gx"), "gy", None)),
        check_vma=False,
    )
```

```python
import functools

import jax
import jax.numpy as jnp
from jax import lax
from jax.experimental import pallas as pl
from jax.experimental.pallas import tpu as pltpu
from jax.sharding import PartitionSpec as P

lift_weight = 0.3
MESH = pl.DeviceIdType.MESH
F32 = jnp.float32
BF16 = jnp.bfloat16
PAD = 8


def kernel(
    n_gx, n_gy,
    source, field, kerr, wave, leaf_ops, transfer_ops,
    upd_v, res_v,
    src_v, fld_v, kerr_v, wave_v, map_v, ops_v, edge_ops, leaf_src, grid, kerr_b, wave_b,
    rims, face_out, face_in, op_out, op_in, edge_out, edge_in,
    row_sems, small_sems, ops_sems, edge_sems,
    face_send, face_recv, op_send, op_recv, halo_send, halo_recv,
):
    x_points, y_points, columns = src_v.shape
    leaves_x, leaves_y, leaf_pts, _ = ops_v.shape
    q = x_points // leaves_x
    half = y_points // 2
    last = leaves_x - 1
    me = lax.axis_index("gx")
    col = lax.axis_index("gy")

    small = [
        pltpu.make_async_copy(kerr, kerr_v, small_sems.at[0]),
        pltpu.make_async_copy(wave, wave_v, small_sems.at[1]),
        pltpu.make_async_copy(transfer_ops.at[0], map_v, small_sems.at[2]),
    ]
    for c in small:
        c.start()
    order = [0, last] + list(range(1, last))
    rows, edges, ops = {}, [], {}
    for a in order:
        span = pl.ds(a * q, q)
        rows[a] = (
            pltpu.make_async_copy(source.at[span], src_v.at[span], row_sems.at[0, a]),
            pltpu.make_async_copy(field.at[span], fld_v.at[span], row_sems.at[1, a]),
        )
    for i, (a, first) in enumerate(((0, 0), (last, leaf_pts - q))):
        edges.append(
            pltpu.make_async_copy(
                leaf_ops.at[a, :, pl.ds(first, q), :], edge_ops.at[i], edge_sems.at[i]
            )
        )
    for a in order:
        ops[a] = pltpu.make_async_copy(leaf_ops.at[a], ops_v.at[a], ops_sems.at[a])
    for a in order[:2]:
        rows[a][0].start()
        rows[a][1].start()
    for c in edges:
        c.start()
    for a in order[2:]:
        rows[a][0].start()
        rows[a][1].start()
    for a in order:
        ops[a].start()

    barrier = pltpu.get_barrier_semaphore()

    def greet(p, carry):
        @pl.when(p != me)
        def _():
            pl.semaphore_signal(barrier, inc=1, device_id={"gx": p}, device_id_type=MESH)

        return carry

    lax.fori_loop(0, n_gx, greet, 0)

    @pl.when(col > 0)
    def _():
        pl.semaphore_signal(barrier, inc=1, device_id={"gy": col - 1}, device_id_type=MESH)

    @pl.when(col < n_gy - 1)
    def _():
        pl.semaphore_signal(barrier, inc=1, device_id={"gy": col + 1}, device_id_type=MESH)

    partners = (n_gx - 1) + jnp.where(col > 0, 1, 0) + jnp.where(col < n_gy - 1, 1, 0)

    for c in small:
        c.wait()
    coeff = jnp.transpose(jnp.concatenate([kerr_v[...], wave_v[...]], axis=0))
    own = map_v[...]
    own_t = jnp.transpose(own)
    for i, m in enumerate((own, own_t)):
        op_out[i] = jnp.concatenate([m[:half], m[half:]], axis=1).astype(BF16)

    def face_copy(side, slot, p):
        return pltpu.make_async_remote_copy(
            src_ref=face_out.at[side],
            dst_ref=face_in.at[slot],
            send_sem=face_send.at[p],
            recv_sem=face_recv.at[slot],
            device_id={"gx": p},
            device_id_type=MESH,
        )

    def op_copy(side, slot, p):
        return pltpu.make_async_remote_copy(
            src_ref=op_out.at[side],
            dst_ref=op_in.at[slot],
            send_sem=op_send.at[p],
            recv_sem=op_recv.at[slot],
            device_id={"gx": p},
            device_id_type=MESH,
        )

    def run(low, high, body):
        def step(p, carry):
            body(p)
            return carry

        lax.fori_loop(low, high, step, 0)

    inner = jnp.logical_and(me > 0, me < n_gx - 1)
    pl.semaphore_wait(barrier, partners)

    @pl.when(inner)
    def _():
        run(me + 1, n_gx, lambda p: op_copy(0, me, p).start())
        run(0, me, lambda p: op_copy(1, me, p).start())

    def leaf_row(a):
        rows[a][0].wait()
        rows[a][1].wait()
        for i in range(q):
            x = a * q + i
            k = jnp.broadcast_to(coeff[:, x : x + 1], (y_points, columns))
            kerr_b[x] = k
            f = fld_v[x].astype(F32)
            s = (src_v[x].astype(F32) - k * f * f * f).astype(BF16)
            for b in range(leaves_y):
                leaf_src[a, b, i * q : (i + 1) * q, :] = s[b * q : (b + 1) * q]

    for i, a in enumerate((0, last)):
        if i == 0 or last > 0:
            leaf_row(a)
        edges[i].wait()
        for b in range(leaves_y):
            face_out[1 - i, b * q : (b + 1) * q, :] = jnp.dot(
                edge_ops[i, b], leaf_src[a, b], preferred_element_type=F32
            ).astype(BF16)
    run(me + 1, n_gx, lambda p: face_copy(0, me, p).start())
    run(0, me, lambda p: face_copy(1, me, p).start())

    for a in order[2:]:
        leaf_row(a)
    for a in order:
        ops[a].wait()
        for b in range(leaves_y):
            solved = jnp.dot(ops_v[a, b], leaf_src[a, b], preferred_element_type=F32)
            for i in range(q):
                grid[1 + a * q + i, PAD + b * q : PAD + (b + 1) * q, :] = solved[i * q : (i + 1) * q]
    for x in range(x_points):
        wave_b[x] = jnp.broadcast_to(
            coeff[:, x_points + x : x_points + x + 1] - 4.0, (y_points, columns)
        )
    zero_row = jnp.zeros((1, columns), F32)
    for x in range(x_points):
        grid[1 + x, PAD - 1 : PAD, :] = zero_row
        grid[1 + x, PAD + y_points : PAD + y_points + 1, :] = zero_row
    low_edge = jnp.concatenate([grid[1 + x, PAD : PAD + 1, :] for x in range(x_points)], axis=0)
    high_edge = jnp.concatenate(
        [grid[1 + x, PAD + y_points - 1 : PAD + y_points, :] for x in range(x_points)], axis=0
    )

    def apply(packed, state):
        s = state.astype(BF16)
        z = jnp.zeros_like(s)
        wide = jnp.concatenate(
            [jnp.concatenate([s, z], axis=1), jnp.concatenate([z, s], axis=1)], axis=0
        )
        out = jnp.dot(packed, wide, preferred_element_type=F32)
        return jnp.concatenate([out[:, :columns], out[:, columns:]], axis=0)

    zeros = jnp.zeros((y_points, columns), F32)

    def arrived(s):
        face_copy(0, s, s).wait_recv()
        return face_in[s].astype(F32)

    def chain(begin, count, step):
        def first():
            return arrived(begin)

        state = lax.cond(count > 0, first, lambda: zeros)

        def hop(i, carry):
            _, now = carry
            s = begin + step * i
            op_copy(0, s, s).wait_recv()
            nxt = apply(op_in[s], now) + arrived(s)
            return now, nxt

        return lax.fori_loop(1, count, hop, (zeros, state))

    w_before, w = chain(0, me, 1)
    z_after, z = chain(n_gx - 1, n_gx - 1 - me, -1)
    w3, z3 = lift_weight * w, lift_weight * z

    position = lax.broadcasted_iota(jnp.int32, (x_points, columns), 0).astype(F32)
    left_prof = (x_points - position) / x_points
    right_prof = (position + 1.0) / x_points
    for i, (edge, y) in enumerate(((low_edge, 0), (high_edge, y_points - 1))):
        edge_out[i] = (
            edge + (left_prof * w3[y : y + 1, :] + right_prof * z3[y : y + 1, :])
        ).astype(BF16)

    def halo_copy(side, p):
        return pltpu.make_async_remote_copy(
            src_ref=edge_out.at[side],
            dst_ref=edge_in.at[1 - side],
            send_sem=halo_send.at[side],
            recv_sem=halo_recv.at[1 - side],
            device_id={"gy": p},
            device_id_type=MESH,
        )

    @pl.when(col > 0)
    def _():
        halo_copy(0, col - 1).start()

    @pl.when(col < n_gy - 1)
    def _():
        halo_copy(1, col + 1).start()

    tip = 1.0 / x_points
    body = pl.ds(PAD, y_points)

    @pl.when(me > 0)
    def _():
        face = face_in[jnp.maximum(me - 1, 0)].astype(F32)
        z_there = apply(op_out[1], z) + grid[1, body, :]
        there = face + lift_weight * (tip * w_before + z_there)
        grid[0, body, :] = there.astype(BF16).astype(F32)

    @pl.when(me == 0)
    def _():
        grid[0, body, :] = zeros

    @pl.when(me < n_gx - 1)
    def _():
        face = face_in[jnp.minimum(me + 1, n_gx - 1)].astype(F32)
        w_there = apply(op_out[0], w) + grid[x_points, body, :]
        there = face + lift_weight * (w_there + tip * z_after)
        grid[x_points + 1, body, :] = there.astype(BF16).astype(F32)

    @pl.when(me == n_gx - 1)
    def _():
        grid[x_points + 1, body, :] = zeros

    def lift(x, carry):
        at = lax.convert_element_type(x, F32)
        u = grid[1 + x, body, :] + (
            ((x_points - at) / x_points) * w3 + ((at + 1.0) / x_points) * z3
        )
        u = u.astype(BF16)
        upd_v[x] = u
        grid[1 + x, body, :] = u.astype(F32)
        return carry

    lax.fori_loop(0, x_points, lift, 0, unroll=4)

    def finish(x, carry):
        mid = grid[1 + x, body, :]
        near = (grid[x, body, :] + grid[2 + x, body, :]) + (
            grid[1 + x, pl.ds(PAD - 1, y_points), :] + grid[1 + x, pl.ds(PAD + 1, y_points), :]
        )
        factor = wave_b[x] + kerr_b[x] * (mid * mid)
        value = near + (factor * mid - src_v[x].astype(F32))
        rims[0, pl.ds(x, 1), :] = value[:1]
        rims[1, pl.ds(x, 1), :] = value[y_points - 1 :]
        res_v[x] = value.astype(BF16)
        return carry

    lax.fori_loop(0, x_points, finish, 0, unroll=4)

    row = lax.broadcasted_iota(jnp.int32, (q, columns), 0)

    def amend(side, low, at):
        full = rims[side] + edge_in[side].astype(F32)
        for x in range(x_points):
            tile = res_v[x, low : low + q, :].astype(F32)
            new = jnp.where(row == at, full[x : x + 1], tile)
            res_v[x, low : low + q, :] = new.astype(BF16)

    @pl.when(col > 0)
    def _():
        halo_copy(1, col - 1).wait_recv()
        amend(0, 0, 0)

    @pl.when(col < n_gy - 1)
    def _():
        halo_copy(0, col + 1).wait_recv()
        amend(1, y_points - q, q - 1)

    run(me + 1, n_gx, lambda p: face_copy(0, me, p).wait_send())
    run(0, me, lambda p: face_copy(1, me, p).wait_send())

    @pl.when(inner)
    def _():
        run(me + 1, n_gx, lambda p: op_copy(0, me, p).wait_send())
        run(0, me, lambda p: op_copy(1, me, p).wait_send())

    @pl.when(col > 0)
    def _():
        halo_copy(0, col - 1).wait_send()

    @pl.when(col < n_gy - 1)
    def _():
        halo_copy(1, col + 1).wait_send()


def store(upd_v, res_v, updated, residual, sems):
    copies = [
        pltpu.make_async_copy(upd_v, updated, sems.at[0]),
        pltpu.make_async_copy(res_v, residual, sems.at[1]),
    ]
    for c in copies:
        c.start()
    for c in copies:
        c.wait()


def per_device(n_gx, n_gy, source, field, kerr, wave, leaf_ops, transfer_ops):
    x_points, y_points, columns = source.shape
    leaves_x, leaves_y, leaf_pts, _ = leaf_ops.shape
    q = x_points // leaves_x
    grid_shape = (x_points, y_points, columns)
    dma = pltpu.SemaphoreType.DMA
    in_hbm = pl.BlockSpec(memory_space=pltpu.HBM)
    in_vmem = pl.BlockSpec(memory_space=pltpu.VMEM)
    operands = [
        pltpu.with_memory_space_constraint(a, pltpu.HBM)
        for a in (source, field, kerr, wave, leaf_ops, transfer_ops)
    ]
    results = pl.pallas_call(
        functools.partial(kernel, n_gx, n_gy),
        out_shape=[pltpu.VMEM(grid_shape, BF16)] * 2,
        in_specs=[in_hbm] * 6,
        out_specs=[in_vmem] * 2,
        scratch_shapes=[
            pltpu.VMEM(grid_shape, BF16),
            pltpu.VMEM(grid_shape, BF16),
            pltpu.VMEM((x_points, y_points), F32),
            pltpu.VMEM((x_points, y_points), F32),
            pltpu.VMEM((y_points, y_points), F32),
            pltpu.VMEM(leaf_ops.shape, BF16),
            pltpu.VMEM((2, leaves_y, q, leaf_pts), BF16),
            pltpu.VMEM((leaves_x, leaves_y, leaf_pts, columns), BF16),
            pltpu.VMEM((x_points + 2, y_points + 2 * PAD, columns), F32),
            pltpu.VMEM(grid_shape, F32),
            pltpu.VMEM(grid_shape, F32),
            pltpu.VMEM((2, x_points, columns), F32),
            pltpu.VMEM((2, y_points, columns), BF16),
            pltpu.VMEM((n_gx, y_points, columns), BF16),
            pltpu.VMEM((2, y_points // 2, 2 * y_points), BF16),
            pltpu.VMEM((n_gx, y_points // 2, 2 * y_points), BF16),
            pltpu.VMEM((2, x_points, columns), BF16),
            pltpu.VMEM((2, x_points, columns), BF16),
            dma((2, leaves_x)),
            dma((3,)),
            dma((leaves_x,)),
            dma((2,)),
            dma((n_gx,)),
            dma((n_gx,)),
            dma((n_gx,)),
            dma((n_gx,)),
            dma((2,)),
            dma((2,)),
        ],
        compiler_params=pltpu.CompilerParams(
            collective_id=0, has_side_effects=True, vmem_limit_bytes=40 * 1024 * 1024
        ),
        cost_estimate=pl.CostEstimate(
            flops=2 * leaf_ops.size * columns, bytes_accessed=6 << 20, transcendentals=0
        ),
        name="kerr_step",
    )(*operands)
    return pl.pallas_call(
        store,
        out_shape=[pltpu.HBM(grid_shape, BF16)] * 2,
        in_specs=[in_vmem] * 2,
        out_specs=[in_hbm] * 2,
        scratch_shapes=[dma((2,))],
        cost_estimate=pl.CostEstimate(flops=0, bytes_accessed=4 << 20, transcendentals=0),
        name="store_results",
    )(*results)


def solution(mesh):
    return jax.shard_map(
        functools.partial(per_device, mesh.shape["gx"], mesh.shape["gy"]),
        mesh=mesh,
        in_specs=(
            P(("grp", "gx"), "gy", None),
            P(("grp", "gx"), "gy", None),
            P(("grp", "gx"), "gy"),
            P(("grp", "gx"), "gy"),
            P("gx", "gy", None, None),
            P("gx", "gy", None),
        ),
        out_specs=(P(("grp", "gx"), "gy", None), P(("grp", "gx"), "gy", None)),
        check_vma=False,
    )
```

```python
import functools

import jax
import jax.numpy as jnp
from jax import lax
from jax.experimental import pallas as pl
from jax.experimental.pallas import tpu as pltpu
from jax.sharding import PartitionSpec as P

lift_weight = 0.3
MESH = pl.DeviceIdType.MESH
F32 = jnp.float32
BF16 = jnp.bfloat16
PAD = 8


def kernel(
    n_gx, n_gy,
    source, field, kerr, wave, leaf_ops, transfer_ops,
    upd_v, res_v,
    src_v, fld_v, kerr_v, wave_v, map_v, ops_v, edge_ops, leaf_src, grid, kerr_b, wave_b,
    rims, face_out, face_in, op_out, op_in, edge_out, edge_in,
    row_sems, small_sems, ops_sems, edge_sems,
    face_send, face_recv, op_send, op_recv, halo_send, halo_recv,
):
    x_points, y_points, columns = src_v.shape
    leaves_x, leaves_y, leaf_pts, _ = ops_v.shape
    q = x_points // leaves_x
    half = y_points // 2
    last = leaves_x - 1
    me = lax.axis_index("gx")
    col = lax.axis_index("gy")

    pitch = y_points + 2 * PAD

    def line(x, low=0, size=y_points):
        start = pl.multiple_of((1 + x) * pitch, 8) + PAD
        return pl.ds(start + low, size)

    def down(y):
        return pl.ds(pitch + PAD + y, x_points, stride=pitch)

    small = [
        pltpu.make_async_copy(kerr, kerr_v, small_sems.at[0]),
        pltpu.make_async_copy(wave, wave_v, small_sems.at[1]),
        pltpu.make_async_copy(transfer_ops.at[0], map_v, small_sems.at[2]),
    ]
    for c in small:
        c.start()
    order = [0, last] + list(range(1, last))
    rows, edges, ops = {}, [], {}
    for a in order:
        span = pl.ds(a * q, q)
        rows[a] = (
            pltpu.make_async_copy(source.at[span], src_v.at[span], row_sems.at[0, a]),
            pltpu.make_async_copy(field.at[span], fld_v.at[span], row_sems.at[1, a]),
        )
    for i, (a, first) in enumerate(((0, 0), (last, leaf_pts - q))):
        edges.append(
            pltpu.make_async_copy(
                leaf_ops.at[a, :, pl.ds(first, q), :], edge_ops.at[i], edge_sems.at[i]
            )
        )
    for a in order:
        ops[a] = pltpu.make_async_copy(leaf_ops.at[a], ops_v.at[a], ops_sems.at[a])
    for a in order[:2]:
        rows[a][0].start()
        rows[a][1].start()
    for c in edges:
        c.start()
    for a in order[2:]:
        rows[a][0].start()
        rows[a][1].start()
    for a in order:
        ops[a].start()

    barrier = pltpu.get_barrier_semaphore()

    def greet(p, carry):
        @pl.when(p != me)
        def _():
            pl.semaphore_signal(barrier, inc=1, device_id={"gx": p}, device_id_type=MESH)

        return carry

    lax.fori_loop(0, n_gx, greet, 0)

    @pl.when(col > 0)
    def _():
        pl.semaphore_signal(barrier, inc=1, device_id={"gy": col - 1}, device_id_type=MESH)

    @pl.when(col < n_gy - 1)
    def _():
        pl.semaphore_signal(barrier, inc=1, device_id={"gy": col + 1}, device_id_type=MESH)

    partners = (n_gx - 1) + jnp.where(col > 0, 1, 0) + jnp.where(col < n_gy - 1, 1, 0)

    for c in small:
        c.wait()
    coeff = jnp.transpose(jnp.concatenate([kerr_v[...], wave_v[...] - 4.0], axis=0))
    own = map_v[...]
    own_t = jnp.transpose(own)
    for i, m in enumerate((own, own_t)):
        op_out[i] = jnp.concatenate([m[:half], m[half:]], axis=1).astype(BF16)

    def face_copy(side, slot, p):
        return pltpu.make_async_remote_copy(
            src_ref=face_out.at[side],
            dst_ref=face_in.at[slot],
            send_sem=face_send.at[p],
            recv_sem=face_recv.at[slot],
            device_id={"gx": p},
            device_id_type=MESH,
        )

    def op_copy(side, slot, p):
        return pltpu.make_async_remote_copy(
            src_ref=op_out.at[side],
            dst_ref=op_in.at[slot],
            send_sem=op_send.at[p],
            recv_sem=op_recv.at[slot],
            device_id={"gx": p},
            device_id_type=MESH,
        )

    def run(low, high, body):
        def step(p, carry):
            body(p)
            return carry

        lax.fori_loop(low, high, step, 0)

    inner = jnp.logical_and(me > 0, me < n_gx - 1)
    pl.semaphore_wait(barrier, partners)

    @pl.when(inner)
    def _():
        run(me + 1, n_gx, lambda p: op_copy(0, me, p).start())
        run(0, me, lambda p: op_copy(1, me, p).start())

    def leaf_row(a):
        for i in range(q):
            x = a * q + i
            k = jnp.broadcast_to(coeff[:, x : x + 1], (y_points, columns))
            kerr_b[x] = k
            f = fld_v[x].astype(F32)
            s = (src_v[x].astype(F32) - k * f * f * f).astype(BF16)
            for b in range(leaves_y):
                leaf_src[a, b, i * q : (i + 1) * q, :] = s[b * q : (b + 1) * q]

    for a in order[:2]:
        rows[a][0].wait()
        rows[a][1].wait()
    for c in edges:
        c.wait()
    for i, a in enumerate((0, last)):
        if i == 0 or last > 0:
            leaf_row(a)
        for b in range(leaves_y):
            face_out[1 - i, b * q : (b + 1) * q, :] = jnp.dot(
                edge_ops[i, b], leaf_src[a, b], preferred_element_type=F32
            ).astype(BF16)
    run(me + 1, n_gx, lambda p: face_copy(0, me, p).start())
    run(0, me, lambda p: face_copy(1, me, p).start())

    for a in order[2:]:
        rows[a][0].wait()
        rows[a][1].wait()
    for a in order:
        ops[a].wait()
    for a in order:
        if a not in order[:2]:
            leaf_row(a)
        for b in range(leaves_y):
            solved = jnp.dot(ops_v[a, b], leaf_src[a, b], preferred_element_type=F32)
            for i in range(q):
                grid[line(a * q + i, b * q, q), :] = solved[i * q : (i + 1) * q]
        for x in range(a * q, (a + 1) * q):
            wave_b[x] = jnp.broadcast_to(
                coeff[:, x_points + x : x_points + x + 1], (y_points, columns)
            )
    blank = jnp.zeros((x_points, columns), F32)
    grid[down(-1), :] = blank
    grid[down(y_points), :] = blank
    low_edge = grid[down(0), :]
    high_edge = grid[down(y_points - 1), :]

    def apply(packed, state):
        s = state.astype(BF16)
        z = jnp.zeros_like(s)
        wide = jnp.concatenate(
            [jnp.concatenate([s, z], axis=1), jnp.concatenate([z, s], axis=1)], axis=0
        )
        out = jnp.dot(packed, wide, preferred_element_type=F32)
        return jnp.concatenate([out[:, :columns], out[:, columns:]], axis=0)

    zeros = jnp.zeros((y_points, columns), F32)

    def arrived(s):
        face_copy(0, s, s).wait_recv()
        return face_in[s].astype(F32)

    def chain(begin, count, step):
        def first():
            return arrived(begin)

        state = lax.cond(count > 0, first, lambda: zeros)

        def hop(i, carry):
            _, now = carry
            s = begin + step * i
            op_copy(0, s, s).wait_recv()
            nxt = apply(op_in[s], now) + arrived(s)
            return now, nxt

        return lax.fori_loop(1, count, hop, (zeros, state))

    w_before, w = chain(0, me, 1)
    z_after, z = chain(n_gx - 1, n_gx - 1 - me, -1)
    w3, z3 = lift_weight * w, lift_weight * z

    position = lax.broadcasted_iota(jnp.int32, (x_points, columns), 0).astype(F32)
    left_prof = (x_points - position) / x_points
    right_prof = (position + 1.0) / x_points
    for i, (edge, y) in enumerate(((low_edge, 0), (high_edge, y_points - 1))):
        edge_out[i] = (
            edge + (left_prof * w3[y : y + 1, :] + right_prof * z3[y : y + 1, :])
        ).astype(BF16)

    def halo_copy(side, p):
        return pltpu.make_async_remote_copy(
            src_ref=edge_out.at[side],
            dst_ref=edge_in.at[1 - side],
            send_sem=halo_send.at[side],
            recv_sem=halo_recv.at[1 - side],
            device_id={"gy": p},
            device_id_type=MESH,
        )

    @pl.when(col > 0)
    def _():
        halo_copy(0, col - 1).start()

    @pl.when(col < n_gy - 1)
    def _():
        halo_copy(1, col + 1).start()

    tip = 1.0 / x_points

    @pl.when(me > 0)
    def _():
        face = face_in[jnp.maximum(me - 1, 0)].astype(F32)
        z_there = apply(op_out[1], z) + grid[line(0), :]
        there = face + lift_weight * (tip * w_before + z_there)
        grid[line(-1), :] = there.astype(BF16).astype(F32)

    @pl.when(me == 0)
    def _():
        grid[line(-1), :] = zeros

    @pl.when(me < n_gx - 1)
    def _():
        face = face_in[jnp.minimum(me + 1, n_gx - 1)].astype(F32)
        w_there = apply(op_out[0], w) + grid[line(x_points - 1), :]
        there = face + lift_weight * (w_there + tip * z_after)
        grid[line(x_points), :] = there.astype(BF16).astype(F32)

    @pl.when(me == n_gx - 1)
    def _():
        grid[line(x_points), :] = zeros

    def lift(x, carry):
        at = lax.convert_element_type(x, F32)
        u = grid[line(x), :] + (
            ((x_points - at) / x_points) * w3 + ((at + 1.0) / x_points) * z3
        )
        u = u.astype(BF16)
        upd_v[x] = u
        grid[line(x), :] = u.astype(F32)
        return carry

    lax.fori_loop(0, x_points, lift, 0, unroll=4)

    block = 4

    def finish(i, carry):
        x = i * block
        for low in range(0, y_points, q):
            part = slice(low, low + q)
            lines = [grid[line(x + j, low, q), :] for j in range(-1, block + 1)]
            for j in range(block):
                mid = lines[j + 1]
                near = (lines[j] + lines[j + 2]) + (
                    grid[line(x + j, low - 1, q), :] + grid[line(x + j, low + 1, q), :]
                )
                factor = wave_b[x + j, part, :] + kerr_b[x + j, part, :] * (mid * mid)
                value = near + (factor * mid - src_v[x + j, part, :].astype(F32))
                if low == 0:
                    rims[0, pl.ds(x + j, 1), :] = value[:1]
                if low + q == y_points:
                    rims[1, pl.ds(x + j, 1), :] = value[q - 1 :]
                res_v[x + j, part, :] = value.astype(BF16)
        return carry

    lax.fori_loop(0, x_points // block, finish, 0)

    row = lax.broadcasted_iota(jnp.int32, (q, columns), 0)

    def amend(side, low, at):
        rims[side] = rims[side] + edge_in[side].astype(F32)
        for x in range(x_points):
            tile = res_v[x, low : low + q, :].astype(F32)
            full = jnp.broadcast_to(rims[side, x : x + 1, :], (q, columns))
            res_v[x, low : low + q, :] = jnp.where(row == at, full, tile).astype(BF16)

    @pl.when(col > 0)
    def _():
        halo_copy(1, col - 1).wait_recv()
        amend(0, 0, 0)

    @pl.when(col < n_gy - 1)
    def _():
        halo_copy(0, col + 1).wait_recv()
        amend(1, y_points - q, q - 1)

    run(me + 1, n_gx, lambda p: face_copy(0, me, p).wait_send())
    run(0, me, lambda p: face_copy(1, me, p).wait_send())

    @pl.when(inner)
    def _():
        run(me + 1, n_gx, lambda p: op_copy(0, me, p).wait_send())
        run(0, me, lambda p: op_copy(1, me, p).wait_send())

    @pl.when(col > 0)
    def _():
        halo_copy(0, col - 1).wait_send()

    @pl.when(col < n_gy - 1)
    def _():
        halo_copy(1, col + 1).wait_send()


def store(upd_v, res_v, updated, residual, sems):
    pieces = sems.shape[1]
    rows = upd_v.shape[0] // pieces
    copies = []
    for i in range(pieces):
        span = pl.ds(i * rows, rows)
        copies.append(pltpu.make_async_copy(upd_v.at[span], updated.at[span], sems.at[0, i]))
        copies.append(pltpu.make_async_copy(res_v.at[span], residual.at[span], sems.at[1, i]))
    for c in copies:
        c.start()
    for c in copies:
        c.wait()


def per_device(n_gx, n_gy, source, field, kerr, wave, leaf_ops, transfer_ops):
    x_points, y_points, columns = source.shape
    leaves_x, leaves_y, leaf_pts, _ = leaf_ops.shape
    q = x_points // leaves_x
    grid_shape = (x_points, y_points, columns)
    dma = pltpu.SemaphoreType.DMA
    in_hbm = pl.BlockSpec(memory_space=pltpu.HBM)
    in_vmem = pl.BlockSpec(memory_space=pltpu.VMEM)
    operands = [
        pltpu.with_memory_space_constraint(a, pltpu.HBM)
        for a in (source, field, kerr, wave, leaf_ops, transfer_ops)
    ]
    results = pl.pallas_call(
        functools.partial(kernel, n_gx, n_gy),
        out_shape=[pltpu.VMEM(grid_shape, BF16)] * 2,
        in_specs=[in_hbm] * 6,
        out_specs=[in_vmem] * 2,
        scratch_shapes=[
            pltpu.VMEM(grid_shape, BF16),
            pltpu.VMEM(grid_shape, BF16),
            pltpu.VMEM((x_points, y_points), F32),
            pltpu.VMEM((x_points, y_points), F32),
            pltpu.VMEM((y_points, y_points), F32),
            pltpu.VMEM(leaf_ops.shape, BF16),
            pltpu.VMEM((2, leaves_y, q, leaf_pts), BF16),
            pltpu.VMEM((leaves_x, leaves_y, leaf_pts, columns), BF16),
            pltpu.VMEM(((x_points + 2) * (y_points + 2 * PAD), columns), F32),
            pltpu.VMEM(grid_shape, F32),
            pltpu.VMEM(grid_shape, F32),
            pltpu.VMEM((2, x_points, columns), F32),
            pltpu.VMEM((2, y_points, columns), BF16),
            pltpu.VMEM((n_gx, y_points, columns), BF16),
            pltpu.VMEM((2, y_points // 2, 2 * y_points), BF16),
            pltpu.VMEM((n_gx, y_points // 2, 2 * y_points), BF16),
            pltpu.VMEM((2, x_points, columns), BF16),
            pltpu.VMEM((2, x_points, columns), BF16),
            dma((2, leaves_x)),
            dma((3,)),
            dma((leaves_x,)),
            dma((2,)),
            dma((n_gx,)),
            dma((n_gx,)),
            dma((n_gx,)),
            dma((n_gx,)),
            dma((2,)),
            dma((2,)),
        ],
        compiler_params=pltpu.CompilerParams(
            collective_id=0, has_side_effects=True, vmem_limit_bytes=40 * 1024 * 1024
        ),
        cost_estimate=pl.CostEstimate(
            flops=2 * leaf_ops.size * columns, bytes_accessed=6 << 20, transcendentals=0
        ),
        name="kerr_step",
    )(*operands)
    return pl.pallas_call(
        store,
        out_shape=[pltpu.HBM(grid_shape, BF16)] * 2,
        in_specs=[pl.BlockSpec(memory_space=pl.ANY)] * 2,
        out_specs=[in_hbm] * 2,
        scratch_shapes=[dma((2, leaves_x))],
        compiler_params=pltpu.CompilerParams(vmem_limit_bytes=1024 * 1024),
        cost_estimate=pl.CostEstimate(flops=0, bytes_accessed=4 << 20, transcendentals=0),
        name="store_results",
    )(*results)


def solution(mesh):
    return jax.shard_map(
        functools.partial(per_device, mesh.shape["gx"], mesh.shape["gy"]),
        mesh=mesh,
        in_specs=(
            P(("grp", "gx"), "gy", None),
            P(("grp", "gx"), "gy", None),
            P(("grp", "gx"), "gy"),
            P(("grp", "gx"), "gy"),
            P("gx", "gy", None, None),
            P("gx", "gy", None),
        ),
        out_specs=(P(("grp", "gx"), "gy", None), P(("grp", "gx"), "gy", None)),
        check_vma=False,
    )
```

```python
import functools

import jax
import jax.numpy as jnp
from jax import lax
from jax.experimental import pallas as pl
from jax.experimental.pallas import tpu as pltpu
from jax.sharding import PartitionSpec as P

lift_weight = 0.3
MESH = pl.DeviceIdType.MESH
F32 = jnp.float32
BF16 = jnp.bfloat16
PAD = 8


def kernel(
    n_gx, n_gy,
    source, field, kerr, wave, leaf_ops, transfer_ops,
    upd_v, res_v, rims,
    src_v, fld_v, kerr_v, wave_v, map_v, ops_v, edge_ops, leaf_src, grid, kerr_b, wave_b,
    face_out, face_in, op_out, op_in, edge_out, edge_in,
    row_sems, small_sems, ops_sems, edge_sems,
    face_send, face_recv, op_send, op_recv, halo_send, halo_recv,
):
    x_points, y_points, columns = src_v.shape
    leaves_x, leaves_y, leaf_pts, _ = ops_v.shape
    q = x_points // leaves_x
    half = y_points // 2
    last = leaves_x - 1
    me = lax.axis_index("gx")
    col = lax.axis_index("gy")

    pitch = y_points + 2 * PAD

    def line(x, low=0, size=y_points):
        start = pl.multiple_of((1 + x) * pitch, 8) + PAD
        return pl.ds(start + low, size)

    def down(y):
        return pl.ds(pitch + PAD + y, x_points, stride=pitch)

    small = [
        pltpu.make_async_copy(kerr, kerr_v, small_sems.at[0]),
        pltpu.make_async_copy(wave, wave_v, small_sems.at[1]),
        pltpu.make_async_copy(transfer_ops.at[0], map_v, small_sems.at[2]),
    ]
    for c in small:
        c.start()
    order = [0, last] + list(range(1, last))
    rows, edges, ops = {}, [], {}
    for a in order:
        span = pl.ds(a * q, q)
        rows[a] = (
            pltpu.make_async_copy(source.at[span], src_v.at[span], row_sems.at[0, a]),
            pltpu.make_async_copy(field.at[span], fld_v.at[span], row_sems.at[1, a]),
        )
    for i, (a, first) in enumerate(((0, 0), (last, leaf_pts - q))):
        edges.append(
            pltpu.make_async_copy(
                leaf_ops.at[a, :, pl.ds(first, q), :], edge_ops.at[i], edge_sems.at[i]
            )
        )
    for a in order:
        ops[a] = pltpu.make_async_copy(leaf_ops.at[a], ops_v.at[a], ops_sems.at[a])
    for a in order[:2]:
        rows[a][0].start()
        rows[a][1].start()
    for c in edges:
        c.start()
    for a in order[2:]:
        rows[a][0].start()
        rows[a][1].start()
    for a in order:
        ops[a].start()

    barrier = pltpu.get_barrier_semaphore()

    def greet(p, carry):
        @pl.when(p != me)
        def _():
            pl.semaphore_signal(barrier, inc=1, device_id={"gx": p}, device_id_type=MESH)

        return carry

    lax.fori_loop(0, n_gx, greet, 0)

    @pl.when(col > 0)
    def _():
        pl.semaphore_signal(barrier, inc=1, device_id={"gy": col - 1}, device_id_type=MESH)

    @pl.when(col < n_gy - 1)
    def _():
        pl.semaphore_signal(barrier, inc=1, device_id={"gy": col + 1}, device_id_type=MESH)

    partners = (n_gx - 1) + jnp.where(col > 0, 1, 0) + jnp.where(col < n_gy - 1, 1, 0)

    for c in small:
        c.wait()
    coeff = jnp.transpose(jnp.concatenate([kerr_v[...], wave_v[...] - 4.0], axis=0))
    own = map_v[...]
    own_t = jnp.transpose(own)
    for i, m in enumerate((own, own_t)):
        op_out[i] = jnp.concatenate([m[:half], m[half:]], axis=1).astype(BF16)

    def face_copy(side, slot, p):
        return pltpu.make_async_remote_copy(
            src_ref=face_out.at[side],
            dst_ref=face_in.at[slot],
            send_sem=face_send.at[p],
            recv_sem=face_recv.at[slot],
            device_id={"gx": p},
            device_id_type=MESH,
        )

    def op_copy(side, slot, p):
        return pltpu.make_async_remote_copy(
            src_ref=op_out.at[side],
            dst_ref=op_in.at[slot],
            send_sem=op_send.at[p],
            recv_sem=op_recv.at[slot],
            device_id={"gx": p},
            device_id_type=MESH,
        )

    def run(low, high, body):
        def step(p, carry):
            body(p)
            return carry

        lax.fori_loop(low, high, step, 0)

    inner = jnp.logical_and(me > 0, me < n_gx - 1)
    pl.semaphore_wait(barrier, partners)

    @pl.when(inner)
    def _():
        run(me + 1, n_gx, lambda p: op_copy(0, me, p).start())
        run(0, me, lambda p: op_copy(1, me, p).start())

    def leaf_row(a):
        for i in range(q):
            x = a * q + i
            k = jnp.broadcast_to(coeff[:, x : x + 1], (y_points, columns))
            kerr_b[x] = k
            f = fld_v[x].astype(F32)
            s = (src_v[x].astype(F32) - k * f * f * f).astype(BF16)
            for b in range(leaves_y):
                leaf_src[a, b, i * q : (i + 1) * q, :] = s[b * q : (b + 1) * q]

    for a in order[:2]:
        rows[a][0].wait()
        rows[a][1].wait()
    for c in edges:
        c.wait()
    for i, a in enumerate((0, last)):
        if i == 0 or last > 0:
            leaf_row(a)
        for b in range(leaves_y):
            face_out[1 - i, b * q : (b + 1) * q, :] = jnp.dot(
                edge_ops[i, b], leaf_src[a, b], preferred_element_type=F32
            ).astype(BF16)
    run(me + 1, n_gx, lambda p: face_copy(0, me, p).start())
    run(0, me, lambda p: face_copy(1, me, p).start())

    for a in order[2:]:
        rows[a][0].wait()
        rows[a][1].wait()
    for a in order:
        ops[a].wait()
    def solve(a, b):
        solved = jnp.dot(ops_v[a, b], leaf_src[a, b], preferred_element_type=F32)
        for i in range(q):
            grid[line(a * q + i, b * q, q), :] = solved[i * q : (i + 1) * q]

    for a in order:
        if a not in order[:2]:
            leaf_row(a)
        for b in sorted({0, leaves_y - 1}):
            solve(a, b)
    blank = jnp.zeros((x_points, columns), F32)
    grid[down(-1), :] = blank
    grid[down(y_points), :] = blank
    low_edge = grid[down(0), :]
    high_edge = grid[down(y_points - 1), :]

    def apply(packed, state):
        s = state.astype(BF16)
        z = jnp.zeros_like(s)
        wide = jnp.concatenate(
            [jnp.concatenate([s, z], axis=1), jnp.concatenate([z, s], axis=1)], axis=0
        )
        out = jnp.dot(packed, wide, preferred_element_type=F32)
        return jnp.concatenate([out[:, :columns], out[:, columns:]], axis=0)

    zeros = jnp.zeros((y_points, columns), F32)

    def arrived(s):
        face_copy(0, s, s).wait_recv()
        return face_in[s].astype(F32)

    def chain(begin, count, step):
        def first():
            return arrived(begin)

        state = lax.cond(count > 0, first, lambda: zeros)

        def hop(i, carry):
            _, now = carry
            s = begin + step * i
            op_copy(0, s, s).wait_recv()
            nxt = apply(op_in[s], now) + arrived(s)
            return now, nxt

        return lax.fori_loop(1, count, hop, (zeros, state))

    w_before, w = chain(0, me, 1)
    z_after, z = chain(n_gx - 1, n_gx - 1 - me, -1)
    w3, z3 = lift_weight * w, lift_weight * z

    position = lax.broadcasted_iota(jnp.int32, (x_points, columns), 0).astype(F32)
    left_prof = (x_points - position) / x_points
    right_prof = (position + 1.0) / x_points
    for i, (edge, y) in enumerate(((low_edge, 0), (high_edge, y_points - 1))):
        edge_out[i] = (
            edge + (left_prof * w3[y : y + 1, :] + right_prof * z3[y : y + 1, :])
        ).astype(BF16)

    def halo_copy(side, p):
        return pltpu.make_async_remote_copy(
            src_ref=edge_out.at[side],
            dst_ref=edge_in.at[1 - side],
            send_sem=halo_send.at[side],
            recv_sem=halo_recv.at[1 - side],
            device_id={"gy": p},
            device_id_type=MESH,
        )

    @pl.when(col > 0)
    def _():
        halo_copy(0, col - 1).start()

    @pl.when(col < n_gy - 1)
    def _():
        halo_copy(1, col + 1).start()

    for a in order:
        for b in range(1, leaves_y - 1):
            solve(a, b)
        for x in range(a * q, (a + 1) * q):
            wave_b[x] = jnp.broadcast_to(
                coeff[:, x_points + x : x_points + x + 1], (y_points, columns)
            )

    tip = 1.0 / x_points

    @pl.when(me > 0)
    def _():
        face = face_in[jnp.maximum(me - 1, 0)].astype(F32)
        z_there = apply(op_out[1], z) + grid[line(0), :]
        there = face + lift_weight * (tip * w_before + z_there)
        grid[line(-1), :] = there.astype(BF16).astype(F32)

    @pl.when(me == 0)
    def _():
        grid[line(-1), :] = zeros

    @pl.when(me < n_gx - 1)
    def _():
        face = face_in[jnp.minimum(me + 1, n_gx - 1)].astype(F32)
        w_there = apply(op_out[0], w) + grid[line(x_points - 1), :]
        there = face + lift_weight * (w_there + tip * z_after)
        grid[line(x_points), :] = there.astype(BF16).astype(F32)

    @pl.when(me == n_gx - 1)
    def _():
        grid[line(x_points), :] = zeros

    def lift(x, carry):
        at = lax.convert_element_type(x, F32)
        u = grid[line(x), :] + (
            ((x_points - at) / x_points) * w3 + ((at + 1.0) / x_points) * z3
        )
        u = u.astype(BF16)
        upd_v[x] = u
        grid[line(x), :] = u.astype(F32)
        return carry

    lax.fori_loop(0, x_points, lift, 0, unroll=8)

    block = 4

    def finish(i, carry):
        x = i * block
        for low in range(0, y_points, q):
            part = slice(low, low + q)
            lines = [grid[line(x + j, low, q), :] for j in range(-1, block + 1)]
            for j in range(block):
                mid = lines[j + 1]
                near = (lines[j] + lines[j + 2]) + (
                    grid[line(x + j, low - 1, q), :] + grid[line(x + j, low + 1, q), :]
                )
                factor = wave_b[x + j, part, :] + kerr_b[x + j, part, :] * (mid * mid)
                value = near + (factor * mid - src_v[x + j, part, :].astype(F32))
                if low == 0:
                    rims[0, pl.ds(x + j, 1), :] = value[:1]
                if low + q == y_points:
                    rims[1, pl.ds(x + j, 1), :] = value[q - 1 :]
                res_v[x + j, part, :] = value.astype(BF16)
        return carry

    lax.fori_loop(0, x_points // block, finish, 0, unroll=2)

    @pl.when(col > 0)
    def _():
        halo_copy(1, col - 1).wait_recv()
        rims[0] = rims[0] + edge_in[0].astype(F32)

    @pl.when(col < n_gy - 1)
    def _():
        halo_copy(0, col + 1).wait_recv()
        rims[1] = rims[1] + edge_in[1].astype(F32)

    run(me + 1, n_gx, lambda p: face_copy(0, me, p).wait_send())
    run(0, me, lambda p: face_copy(1, me, p).wait_send())

    @pl.when(inner)
    def _():
        run(me + 1, n_gx, lambda p: op_copy(0, me, p).wait_send())
        run(0, me, lambda p: op_copy(1, me, p).wait_send())

    @pl.when(col > 0)
    def _():
        halo_copy(0, col - 1).wait_send()

    @pl.when(col < n_gy - 1)
    def _():
        halo_copy(1, col + 1).wait_send()


def store(pieces, upd_v, res_v, rims, updated, residual, sides, sems):
    x_points, y_points, columns = upd_v.shape
    q = sides.shape[2]
    rows = x_points // pieces
    inner = pl.ds(q, y_points - 2 * q)
    copies = []

    def send(src, dst):
        copies.append(pltpu.make_async_copy(src, dst, sems.at[len(copies)]))
        copies[-1].start()

    for i in range(pieces):
        span = pl.ds(i * rows, rows)
        send(upd_v.at[span], updated.at[span])
    for i in range(pieces):
        span = pl.ds(i * rows, rows)
        send(res_v.at[span, inner, :], residual.at[span, inner, :])
    row = lax.broadcasted_iota(jnp.int32, (q, columns), 0)
    for side, low, at in ((0, 0, 0), (1, y_points - q, q - 1)):
        for x in range(x_points):
            tile = res_v[x, low : low + q, :].astype(F32)
            full = jnp.broadcast_to(rims[side, x : x + 1, :], (q, columns))
            sides[side, x] = jnp.where(row == at, full, tile).astype(BF16)
        send(sides.at[side], residual.at[:, pl.ds(low, q), :])
    for c in copies:
        c.wait()


def per_device(n_gx, n_gy, source, field, kerr, wave, leaf_ops, transfer_ops):
    x_points, y_points, columns = source.shape
    leaves_x, leaves_y, leaf_pts, _ = leaf_ops.shape
    q = x_points // leaves_x
    grid_shape = (x_points, y_points, columns)
    dma = pltpu.SemaphoreType.DMA
    in_hbm = pl.BlockSpec(memory_space=pltpu.HBM)
    in_vmem = pl.BlockSpec(memory_space=pltpu.VMEM)
    operands = [
        pltpu.with_memory_space_constraint(a, pltpu.HBM)
        for a in (source, field, kerr, wave, leaf_ops, transfer_ops)
    ]
    results = pl.pallas_call(
        functools.partial(kernel, n_gx, n_gy),
        out_shape=[
            pltpu.VMEM(grid_shape, BF16),
            pltpu.VMEM(grid_shape, BF16),
            pltpu.VMEM((2, x_points, columns), F32),
        ],
        in_specs=[in_hbm] * 6,
        out_specs=[in_vmem] * 3,
        scratch_shapes=[
            pltpu.VMEM(grid_shape, BF16),
            pltpu.VMEM(grid_shape, BF16),
            pltpu.VMEM((x_points, y_points), F32),
            pltpu.VMEM((x_points, y_points), F32),
            pltpu.VMEM((y_points, y_points), F32),
            pltpu.VMEM(leaf_ops.shape, BF16),
            pltpu.VMEM((2, leaves_y, q, leaf_pts), BF16),
            pltpu.VMEM((leaves_x, leaves_y, leaf_pts, columns), BF16),
            pltpu.VMEM(((x_points + 2) * (y_points + 2 * PAD), columns), F32),
            pltpu.VMEM(grid_shape, F32),
            pltpu.VMEM(grid_shape, F32),
            pltpu.VMEM((2, y_points, columns), BF16),
            pltpu.VMEM((n_gx, y_points, columns), BF16),
            pltpu.VMEM((2, y_points // 2, 2 * y_points), BF16),
            pltpu.VMEM((n_gx, y_points // 2, 2 * y_points), BF16),
            pltpu.VMEM((2, x_points, columns), BF16),
            pltpu.VMEM((2, x_points, columns), BF16),
            dma((2, leaves_x)),
            dma((3,)),
            dma((leaves_x,)),
            dma((2,)),
            dma((n_gx,)),
            dma((n_gx,)),
            dma((n_gx,)),
            dma((n_gx,)),
            dma((2,)),
            dma((2,)),
        ],
        compiler_params=pltpu.CompilerParams(
            collective_id=0, has_side_effects=True, vmem_limit_bytes=40 * 1024 * 1024
        ),
        cost_estimate=pl.CostEstimate(
            flops=2 * leaf_ops.size * columns, bytes_accessed=6 << 20, transcendentals=0
        ),
        name="kerr_step",
    )(*operands)
    return pl.pallas_call(
        functools.partial(store, leaves_x),
        out_shape=[pltpu.HBM(grid_shape, BF16)] * 2,
        in_specs=[in_vmem] * 3,
        out_specs=[in_hbm] * 2,
        scratch_shapes=[
            pltpu.VMEM((2, x_points, q, columns), BF16),
            dma((2 * leaves_x + 2,)),
        ],
        compiler_params=pltpu.CompilerParams(vmem_limit_bytes=2 * 1024 * 1024),
        cost_estimate=pl.CostEstimate(flops=0, bytes_accessed=4 << 20, transcendentals=0),
        name="store_results",
    )(*results)


def solution(mesh):
    return jax.shard_map(
        functools.partial(per_device, mesh.shape["gx"], mesh.shape["gy"]),
        mesh=mesh,
        in_specs=(
            P(("grp", "gx"), "gy", None),
            P(("grp", "gx"), "gy", None),
            P(("grp", "gx"), "gy"),
            P(("grp", "gx"), "gy"),
            P("gx", "gy", None, None),
            P("gx", "gy", None),
        ),
        out_specs=(P(("grp", "gx"), "gy", None), P(("grp", "gx"), "gy", None)),
        check_vma=False,
    )
```

```python
import functools

import jax
import jax.numpy as jnp
from jax import lax
from jax.experimental import pallas as pl
from jax.experimental.pallas import tpu as pltpu
from jax.sharding import PartitionSpec as P

lift_weight = 0.3
MESH = pl.DeviceIdType.MESH
F32 = jnp.float32
BF16 = jnp.bfloat16
PAD = 8


def kernel(
    n_gx, n_gy,
    source, field, kerr, wave, leaf_ops, transfer_ops,
    upd_v, res_v, rims,
    src_v, fld_v, kerr_v, wave_v, map_v, ops_v, edge_ops, leaf_src, grid, kerr_b, wave_b,
    face_out, face_in, op_out, op_in, edge_out, edge_in,
    row_sems, small_sems, ops_sems, edge_sems,
    face_send, face_recv, op_send, op_recv, halo_send, halo_recv,
):
    x_points, y_points, columns = src_v.shape
    leaves_x, leaves_y, leaf_pts, _ = ops_v.shape
    q = x_points // leaves_x
    half = y_points // 2
    last = leaves_x - 1
    me = lax.axis_index("gx")
    col = lax.axis_index("gy")

    pitch = y_points + 2 * PAD

    def line(x, low=0, size=y_points):
        start = pl.multiple_of((1 + x) * pitch, 8) + PAD
        return pl.ds(start + low, size)

    def down(y):
        return pl.ds(pitch + PAD + y, x_points, stride=pitch)

    barrier = pltpu.get_barrier_semaphore()

    def greet(p, carry):
        @pl.when(p != me)
        def _():
            pl.semaphore_signal(barrier, inc=1, device_id={"gx": p}, device_id_type=MESH)

        return carry

    @pl.when(col > 0)
    def _():
        pl.semaphore_signal(barrier, inc=1, device_id={"gy": col - 1}, device_id_type=MESH)

    @pl.when(col < n_gy - 1)
    def _():
        pl.semaphore_signal(barrier, inc=1, device_id={"gy": col + 1}, device_id_type=MESH)

    partners = (n_gx - 1) + jnp.where(col > 0, 1, 0) + jnp.where(col < n_gy - 1, 1, 0)

    lax.fori_loop(0, n_gx, greet, 0)

    small = [
        pltpu.make_async_copy(kerr, kerr_v, small_sems.at[0]),
        pltpu.make_async_copy(wave, wave_v, small_sems.at[1]),
        pltpu.make_async_copy(transfer_ops.at[0], map_v, small_sems.at[2]),
    ]
    for c in small:
        c.start()
    order = [0, last] + list(range(1, last))
    rows, edges, ops = {}, [], {}
    for a in order:
        span = pl.ds(a * q, q)
        rows[a] = (
            pltpu.make_async_copy(source.at[span], src_v.at[span], row_sems.at[0, a]),
            pltpu.make_async_copy(field.at[span], fld_v.at[span], row_sems.at[1, a]),
        )
    for i, (a, first) in enumerate(((0, 0), (last, leaf_pts - q))):
        edges.append(
            pltpu.make_async_copy(
                leaf_ops.at[a, :, pl.ds(first, q), :], edge_ops.at[i], edge_sems.at[i]
            )
        )
    for a in order:
        ops[a] = pltpu.make_async_copy(leaf_ops.at[a], ops_v.at[a], ops_sems.at[a])
    for a in order[:2]:
        rows[a][0].start()
        rows[a][1].start()
    for c in edges:
        c.start()
    for a in order[2:]:
        rows[a][0].start()
        rows[a][1].start()
    for a in order:
        ops[a].start()

    for c in small:
        c.wait()
    coeff = jnp.transpose(jnp.concatenate([kerr_v[...], wave_v[...] - 4.0], axis=0))
    own = map_v[...]
    own_t = jnp.transpose(own)
    for i, m in enumerate((own, own_t)):
        op_out[i] = jnp.concatenate([m[:half], m[half:]], axis=1).astype(BF16)

    def face_copy(side, slot, p):
        return pltpu.make_async_remote_copy(
            src_ref=face_out.at[side],
            dst_ref=face_in.at[slot],
            send_sem=face_send.at[p],
            recv_sem=face_recv.at[slot],
            device_id={"gx": p},
            device_id_type=MESH,
        )

    def op_copy(side, slot, p):
        return pltpu.make_async_remote_copy(
            src_ref=op_out.at[side],
            dst_ref=op_in.at[slot],
            send_sem=op_send.at[p],
            recv_sem=op_recv.at[slot],
            device_id={"gx": p},
            device_id_type=MESH,
        )

    def run(low, high, body):
        def step(p, carry):
            body(p)
            return carry

        lax.fori_loop(low, high, step, 0)

    inner = jnp.logical_and(me > 0, me < n_gx - 1)
    def leaf_row(a):
        for i in range(q):
            x = a * q + i
            k = jnp.broadcast_to(coeff[:, x : x + 1], (y_points, columns))
            kerr_b[x] = k
            f = fld_v[x].astype(F32)
            s = (src_v[x].astype(F32) - k * f * f * f).astype(BF16)
            for b in range(leaves_y):
                leaf_src[a, b, i * q : (i + 1) * q, :] = s[b * q : (b + 1) * q]

    for a in order[:2]:
        rows[a][0].wait()
        rows[a][1].wait()
    for c in edges:
        c.wait()
    for i, a in enumerate((0, last)):
        if i == 0 or last > 0:
            leaf_row(a)
        for b in range(leaves_y):
            face_out[1 - i, b * q : (b + 1) * q, :] = jnp.dot(
                edge_ops[i, b], leaf_src[a, b], preferred_element_type=F32
            ).astype(BF16)
    pl.semaphore_wait(barrier, partners)
    run(me + 1, n_gx, lambda p: face_copy(0, me, p).start())
    run(0, me, lambda p: face_copy(1, me, p).start())

    @pl.when(inner)
    def _():
        run(me + 1, n_gx, lambda p: op_copy(0, me, p).start())
        run(0, me, lambda p: op_copy(1, me, p).start())

    for a in order[2:]:
        rows[a][0].wait()
        rows[a][1].wait()
    for a in order:
        ops[a].wait()
    def solve(a, b):
        solved = jnp.dot(ops_v[a, b], leaf_src[a, b], preferred_element_type=F32)
        for i in range(q):
            grid[line(a * q + i, b * q, q), :] = solved[i * q : (i + 1) * q]

    for a in order:
        if a not in order[:2]:
            leaf_row(a)
        for b in sorted({0, leaves_y - 1}):
            solve(a, b)
    blank = jnp.zeros((x_points, columns), F32)
    grid[down(-1), :] = blank
    grid[down(y_points), :] = blank
    low_edge = grid[down(0), :]
    high_edge = grid[down(y_points - 1), :]

    def inner_leaves():
        for a in order:
            for b in range(1, leaves_y - 1):
                solve(a, b)
            for x in range(a * q, (a + 1) * q):
                wave_b[x] = jnp.broadcast_to(
                    coeff[:, x_points + x : x_points + x + 1], (y_points, columns)
                )

    def apply(packed, state):
        s = state.astype(BF16)
        z = jnp.zeros_like(s)
        wide = jnp.concatenate(
            [jnp.concatenate([s, z], axis=1), jnp.concatenate([z, s], axis=1)], axis=0
        )
        out = jnp.dot(packed, wide, preferred_element_type=F32)
        return jnp.concatenate([out[:, :columns], out[:, columns:]], axis=0)

    zeros = jnp.zeros((y_points, columns), F32)

    def arrived(s):
        face_copy(0, s, s).wait_recv()
        return face_in[s].astype(F32)

    def chain(begin, count, step):
        def first():
            return arrived(begin)

        state = lax.cond(count > 0, first, lambda: zeros)

        def hop(i, carry):
            _, now = carry
            s = begin + step * i
            op_copy(0, s, s).wait_recv()
            nxt = apply(op_in[s], now) + arrived(s)
            return now, nxt

        return lax.fori_loop(1, count, hop, (zeros, state))

    def straight():
        def wait(s):
            face_copy(0, s, s).wait_recv()

            @pl.when(jnp.logical_and(s > 0, s < n_gx - 1))
            def _():
                op_copy(0, s, s).wait_recv()

        run(0, me, wait)
        run(me + 1, n_gx, wait)
        states = []
        for steps, before in (
            (range(n_gx - 1), lambda s: s < me),
            (range(n_gx - 1, 0, -1), lambda s: s > me),
        ):
            prev, now = zeros, zeros
            for s in steps:
                nxt = face_in[s].astype(F32)
                if s != steps[0]:
                    nxt = nxt + apply(op_in[s], now)
                take = before(s)
                prev, now = jnp.where(take, now, prev), jnp.where(take, nxt, now)
            states += [prev, now]
        return states

    if n_gx <= 8:
        w_before, w, z_after, z = straight()
    else:
        w_before, w = chain(0, me, 1)
        z_after, z = chain(n_gx - 1, n_gx - 1 - me, -1)
    z_there = apply(op_out[1], z) + face_out[1].astype(F32)
    w_there = apply(op_out[0], w) + face_out[0].astype(F32)
    inner_leaves()
    w3, z3 = lift_weight * w, lift_weight * z

    position = lax.broadcasted_iota(jnp.int32, (x_points, columns), 0).astype(F32)
    left_prof = (x_points - position) / x_points
    right_prof = (position + 1.0) / x_points
    for i, (edge, y) in enumerate(((low_edge, 0), (high_edge, y_points - 1))):
        edge_out[i] = (
            edge + (left_prof * w3[y : y + 1, :] + right_prof * z3[y : y + 1, :])
        ).astype(BF16)

    def halo_copy(side, p):
        return pltpu.make_async_remote_copy(
            src_ref=edge_out.at[side],
            dst_ref=edge_in.at[1 - side],
            send_sem=halo_send.at[side],
            recv_sem=halo_recv.at[1 - side],
            device_id={"gy": p},
            device_id_type=MESH,
        )

    @pl.when(col > 0)
    def _():
        halo_copy(0, col - 1).start()

    @pl.when(col < n_gy - 1)
    def _():
        halo_copy(1, col + 1).start()

    tip = 1.0 / x_points

    face = face_in[jnp.maximum(me - 1, 0)].astype(F32)
    there = face + lift_weight * (tip * w_before + z_there)
    grid[line(-1), :] = jnp.where(me > 0, there.astype(BF16).astype(F32), zeros)
    face = face_in[jnp.minimum(me + 1, n_gx - 1)].astype(F32)
    there = face + lift_weight * (w_there + tip * z_after)
    grid[line(x_points), :] = jnp.where(me < n_gx - 1, there.astype(BF16).astype(F32), zeros)

    def lift(x, carry):
        at = lax.convert_element_type(x, F32)
        u = grid[line(x), :] + (
            ((x_points - at) / x_points) * w3 + ((at + 1.0) / x_points) * z3
        )
        u = u.astype(BF16)
        upd_v[x] = u
        grid[line(x), :] = u.astype(F32)
        return carry

    lax.fori_loop(0, x_points, lift, 0, unroll=8)

    block = 4

    def finish(i, carry):
        x = i * block
        for low in range(0, y_points, q):
            part = slice(low, low + q)
            lines = [grid[line(x + j, low, q), :] for j in range(-1, block + 1)]
            for j in range(block):
                mid = lines[j + 1]
                near = (lines[j] + lines[j + 2]) + (
                    grid[line(x + j, low - 1, q), :] + grid[line(x + j, low + 1, q), :]
                )
                factor = wave_b[x + j, part, :] + kerr_b[x + j, part, :] * (mid * mid)
                value = near + (factor * mid - src_v[x + j, part, :].astype(F32))
                if low == 0:
                    rims[0, pl.ds(x + j, 1), :] = value[:1]
                if low + q == y_points:
                    rims[1, pl.ds(x + j, 1), :] = value[q - 1 :]
                res_v[x + j, part, :] = value.astype(BF16)
        return carry

    lax.fori_loop(0, x_points // block, finish, 0, unroll=2)

    @pl.when(col > 0)
    def _():
        halo_copy(1, col - 1).wait_recv()
        rims[0] = rims[0] + edge_in[0].astype(F32)

    @pl.when(col < n_gy - 1)
    def _():
        halo_copy(0, col + 1).wait_recv()
        rims[1] = rims[1] + edge_in[1].astype(F32)

    run(me + 1, n_gx, lambda p: face_copy(0, me, p).wait_send())
    run(0, me, lambda p: face_copy(1, me, p).wait_send())

    @pl.when(inner)
    def _():
        run(me + 1, n_gx, lambda p: op_copy(0, me, p).wait_send())
        run(0, me, lambda p: op_copy(1, me, p).wait_send())

    @pl.when(col > 0)
    def _():
        halo_copy(0, col - 1).wait_send()

    @pl.when(col < n_gy - 1)
    def _():
        halo_copy(1, col + 1).wait_send()


def store(pieces, upd_v, res_v, rims, updated, residual, sides, sems):
    x_points, y_points, columns = upd_v.shape
    q = sides.shape[2]
    rows = x_points // pieces
    inner = pl.ds(q, y_points - 2 * q)
    copies = []

    def send(src, dst):
        copies.append(pltpu.make_async_copy(src, dst, sems.at[len(copies)]))
        copies[-1].start()

    for i in range(pieces):
        span = pl.ds(i * rows, rows)
        send(upd_v.at[span], updated.at[span])
    for i in range(pieces):
        span = pl.ds(i * rows, rows)
        send(res_v.at[span, inner, :], residual.at[span, inner, :])
    row = lax.broadcasted_iota(jnp.int32, (q, columns), 0)
    for side, low, at in ((0, 0, 0), (1, y_points - q, q - 1)):
        for x in range(x_points):
            tile = res_v[x, low : low + q, :].astype(F32)
            full = jnp.broadcast_to(rims[side, x : x + 1, :], (q, columns))
            sides[side, x] = jnp.where(row == at, full, tile).astype(BF16)
        send(sides.at[side], residual.at[:, pl.ds(low, q), :])
    for c in copies:
        c.wait()


def per_device(n_gx, n_gy, source, field, kerr, wave, leaf_ops, transfer_ops):
    x_points, y_points, columns = source.shape
    leaves_x, leaves_y, leaf_pts, _ = leaf_ops.shape
    q = x_points // leaves_x
    grid_shape = (x_points, y_points, columns)
    dma = pltpu.SemaphoreType.DMA
    in_hbm = pl.BlockSpec(memory_space=pltpu.HBM)
    in_vmem = pl.BlockSpec(memory_space=pltpu.VMEM)
    operands = [
        pltpu.with_memory_space_constraint(a, pltpu.HBM)
        for a in (source, field, kerr, wave, leaf_ops, transfer_ops)
    ]
    results = pl.pallas_call(
        functools.partial(kernel, n_gx, n_gy),
        out_shape=[
            pltpu.VMEM(grid_shape, BF16),
            pltpu.VMEM(grid_shape, BF16),
            pltpu.VMEM((2, x_points, columns), F32),
        ],
        in_specs=[in_hbm] * 6,
        out_specs=[in_vmem] * 3,
        scratch_shapes=[
            pltpu.VMEM(grid_shape, BF16),
            pltpu.VMEM(grid_shape, BF16),
            pltpu.VMEM((x_points, y_points), F32),
            pltpu.VMEM((x_points, y_points), F32),
            pltpu.VMEM((y_points, y_points), F32),
            pltpu.VMEM(leaf_ops.shape, BF16),
            pltpu.VMEM((2, leaves_y, q, leaf_pts), BF16),
            pltpu.VMEM((leaves_x, leaves_y, leaf_pts, columns), BF16),
            pltpu.VMEM(((x_points + 2) * (y_points + 2 * PAD), columns), F32),
            pltpu.VMEM(grid_shape, F32),
            pltpu.VMEM(grid_shape, F32),
            pltpu.VMEM((2, y_points, columns), BF16),
            pltpu.VMEM((n_gx, y_points, columns), BF16),
            pltpu.VMEM((2, y_points // 2, 2 * y_points), BF16),
            pltpu.VMEM((n_gx, y_points // 2, 2 * y_points), BF16),
            pltpu.VMEM((2, x_points, columns), BF16),
            pltpu.VMEM((2, x_points, columns), BF16),
            dma((2, leaves_x)),
            dma((3,)),
            dma((leaves_x,)),
            dma((2,)),
            dma((n_gx,)),
            dma((n_gx,)),
            dma((n_gx,)),
            dma((n_gx,)),
            dma((2,)),
            dma((2,)),
        ],
        compiler_params=pltpu.CompilerParams(
            collective_id=0, has_side_effects=True, vmem_limit_bytes=40 * 1024 * 1024
        ),
        cost_estimate=pl.CostEstimate(
            flops=2 * leaf_ops.size * columns, bytes_accessed=6 << 20, transcendentals=0
        ),
        name="kerr_step",
    )(*operands)
    return pl.pallas_call(
        functools.partial(store, leaves_x),
        out_shape=[pltpu.HBM(grid_shape, BF16)] * 2,
        in_specs=[in_vmem] * 3,
        out_specs=[in_hbm] * 2,
        scratch_shapes=[
            pltpu.VMEM((2, x_points, q, columns), BF16),
            dma((2 * leaves_x + 2,)),
        ],
        compiler_params=pltpu.CompilerParams(vmem_limit_bytes=2 * 1024 * 1024),
        cost_estimate=pl.CostEstimate(flops=0, bytes_accessed=4 << 20, transcendentals=0),
        name="store_results",
    )(*results)


def solution(mesh):
    return jax.shard_map(
        functools.partial(per_device, mesh.shape["gx"], mesh.shape["gy"]),
        mesh=mesh,
        in_specs=(
            P(("grp", "gx"), "gy", None),
            P(("grp", "gx"), "gy", None),
            P(("grp", "gx"), "gy"),
            P(("grp", "gx"), "gy"),
            P("gx", "gy", None, None),
            P("gx", "gy", None),
        ),
        out_specs=(P(("grp", "gx"), "gy", None), P(("grp", "gx"), "gy", None)),
        check_vma=False,
    )
```

```python
import functools

import jax
import jax.numpy as jnp
from jax import lax
from jax.experimental import pallas as pl
from jax.experimental.pallas import tpu as pltpu
from jax.sharding import PartitionSpec as P

lift_weight = 0.3
MESH = pl.DeviceIdType.MESH
F32 = jnp.float32
BF16 = jnp.bfloat16
PAD = 8


def kernel(
    n_gx, n_gy,
    source, field, kerr, wave, leaf_ops, transfer_ops,
    upd_v, res_v, rims,
    src_v, fld_v, kerr_v, wave_v, map_v, ops_v, edge_ops, leaf_src, grid, kerr_b, wave_b,
    face_out, face_in, op_out, op_in, edge_out, edge_in,
    row_sems, small_sems, ops_sems, edge_sems,
    face_send, face_recv, op_send, op_recv, halo_send, halo_recv,
):
    x_points, y_points, columns = src_v.shape
    leaves_x, leaves_y, leaf_pts, _ = ops_v.shape
    q = x_points // leaves_x
    half = y_points // 2
    last = leaves_x - 1
    me = lax.axis_index("gx")
    col = lax.axis_index("gy")

    pitch = y_points + 2 * PAD

    def line(x, low=0, size=y_points):
        start = pl.multiple_of((1 + x) * pitch, 8) + PAD
        return pl.ds(start + low, size)

    def down(y):
        return pl.ds(pitch + PAD + y, x_points, stride=pitch)

    small = [
        pltpu.make_async_copy(kerr, kerr_v, small_sems.at[0]),
        pltpu.make_async_copy(wave, wave_v, small_sems.at[1]),
        pltpu.make_async_copy(transfer_ops.at[0], map_v, small_sems.at[2]),
    ]
    for c in small:
        c.start()
    order = [0, last] + list(range(1, last))
    rows, edges, ops = {}, [], {}
    for a in order:
        span = pl.ds(a * q, q)
        rows[a] = (
            pltpu.make_async_copy(source.at[span], src_v.at[span], row_sems.at[0, a]),
            pltpu.make_async_copy(field.at[span], fld_v.at[span], row_sems.at[1, a]),
        )
    for i, (a, first) in enumerate(((0, 0), (last, leaf_pts - q))):
        edges.append(
            pltpu.make_async_copy(
                leaf_ops.at[a, :, pl.ds(first, q), :], edge_ops.at[i], edge_sems.at[i]
            )
        )
    for a in order:
        ops[a] = pltpu.make_async_copy(leaf_ops.at[a], ops_v.at[a], ops_sems.at[a])
    for a in order[:2]:
        rows[a][0].start()
        rows[a][1].start()
    for c in edges:
        c.start()
    barrier = pltpu.get_barrier_semaphore()

    def greet(p, carry):
        @pl.when(p != me)
        def _():
            pl.semaphore_signal(barrier, inc=1, device_id={"gx": p}, device_id_type=MESH)

        return carry

    @pl.when(col > 0)
    def _():
        pl.semaphore_signal(barrier, inc=1, device_id={"gy": col - 1}, device_id_type=MESH)

    @pl.when(col < n_gy - 1)
    def _():
        pl.semaphore_signal(barrier, inc=1, device_id={"gy": col + 1}, device_id_type=MESH)

    partners = (n_gx - 1) + jnp.where(col > 0, 1, 0) + jnp.where(col < n_gy - 1, 1, 0)

    lax.fori_loop(0, n_gx, greet, 0)

    for a in order[2:]:
        rows[a][0].start()
        rows[a][1].start()
    for a in order:
        ops[a].start()

    small[0].wait()
    small[1].wait()
    coeff = jnp.transpose(jnp.concatenate([kerr_v[...], wave_v[...] - 4.0], axis=0))

    def face_copy(side, slot, p):
        return pltpu.make_async_remote_copy(
            src_ref=face_out.at[side],
            dst_ref=face_in.at[slot],
            send_sem=face_send.at[p],
            recv_sem=face_recv.at[slot],
            device_id={"gx": p},
            device_id_type=MESH,
        )

    def op_copy(side, slot, p):
        return pltpu.make_async_remote_copy(
            src_ref=op_out.at[side],
            dst_ref=op_in.at[slot],
            send_sem=op_send.at[p],
            recv_sem=op_recv.at[slot],
            device_id={"gx": p},
            device_id_type=MESH,
        )

    def run(low, high, body):
        def step(p, carry):
            body(p)
            return carry

        lax.fori_loop(low, high, step, 0)

    inner = jnp.logical_and(me > 0, me < n_gx - 1)
    def leaf_row(a):
        for i in range(q):
            x = a * q + i
            k = jnp.broadcast_to(coeff[:, x : x + 1], (y_points, columns))
            kerr_b[x] = k
            f = fld_v[x].astype(F32)
            s = (src_v[x].astype(F32) - k * f * f * f).astype(BF16)
            for b in range(leaves_y):
                leaf_src[a, b, i * q : (i + 1) * q, :] = s[b * q : (b + 1) * q]

    for i, a in enumerate((0, last)):
        if i == 0 or last > 0:
            rows[a][0].wait()
            rows[a][1].wait()
            leaf_row(a)
        edges[i].wait()
        for b in range(leaves_y):
            face_out[1 - i, b * q : (b + 1) * q, :] = jnp.dot(
                edge_ops[i, b], leaf_src[a, b], preferred_element_type=F32
            ).astype(BF16)
        if i == 0:
            pl.semaphore_wait(barrier, partners)
            run(0, me, lambda p: face_copy(1, me, p).start())
        else:
            run(me + 1, n_gx, lambda p: face_copy(0, me, p).start())

    small[2].wait()
    own = map_v[...]
    own_t = jnp.transpose(own)
    for i, m in enumerate((own, own_t)):
        op_out[i] = jnp.concatenate([m[:half], m[half:]], axis=1).astype(BF16)

    @pl.when(inner)
    def _():
        run(me + 1, n_gx, lambda p: op_copy(0, me, p).start())
        run(0, me, lambda p: op_copy(1, me, p).start())

    for a in order[2:]:
        rows[a][0].wait()
        rows[a][1].wait()
    for a in order:
        ops[a].wait()
    def solve(a, b):
        solved = jnp.dot(ops_v[a, b], leaf_src[a, b], preferred_element_type=F32)
        for i in range(q):
            grid[line(a * q + i, b * q, q), :] = solved[i * q : (i + 1) * q]

    for a in order:
        if a not in order[:2]:
            leaf_row(a)
        for b in sorted({0, leaves_y - 1}):
            solve(a, b)
    blank = jnp.zeros((x_points, columns), F32)
    grid[down(-1), :] = blank
    grid[down(y_points), :] = blank
    low_edge = grid[down(0), :]
    high_edge = grid[down(y_points - 1), :]

    def inner_leaves(part):
        for a in part:
            for b in range(1, leaves_y - 1):
                solve(a, b)

    def wave_rows(part):
        for a in part:
            for x in range(a * q, (a + 1) * q):
                wave_b[x] = jnp.broadcast_to(
                    coeff[:, x_points + x : x_points + x + 1], (y_points, columns)
                )

    inner_leaves(order[:2])

    def apply(packed, state):
        s = state.astype(BF16)
        z = jnp.zeros_like(s)
        wide = jnp.concatenate(
            [jnp.concatenate([s, z], axis=1), jnp.concatenate([z, s], axis=1)], axis=0
        )
        out = jnp.dot(packed, wide, preferred_element_type=F32)
        return jnp.concatenate([out[:, :columns], out[:, columns:]], axis=0)

    zeros = jnp.zeros((y_points, columns), F32)

    def arrived(s):
        face_copy(0, s, s).wait_recv()
        return face_in[s].astype(F32)

    def chain(begin, count, step):
        def first():
            return arrived(begin)

        state = lax.cond(count > 0, first, lambda: zeros)

        def hop(i, carry):
            _, now = carry
            s = begin + step * i
            op_copy(0, s, s).wait_recv()
            nxt = apply(op_in[s], now) + arrived(s)
            return now, nxt

        return lax.fori_loop(1, count, hop, (zeros, state))

    def straight():
        def wait(s):
            face_copy(0, s, s).wait_recv()

            @pl.when(jnp.logical_and(s > 0, s < n_gx - 1))
            def _():
                op_copy(0, s, s).wait_recv()

        run(0, me, wait)
        run(me + 1, n_gx, wait)
        states = []
        for steps, before in (
            (range(n_gx - 1), lambda s: s < me),
            (range(n_gx - 1, 0, -1), lambda s: s > me),
        ):
            prev, now = zeros, zeros
            for s in steps:
                nxt = face_in[s].astype(F32)
                if s != steps[0]:
                    nxt = nxt + apply(op_in[s], now)
                take = before(s)
                prev, now = jnp.where(take, now, prev), jnp.where(take, nxt, now)
            states += [prev, now]
        return states

    if n_gx <= 8:
        w_before, w, z_after, z = straight()
    else:
        w_before, w = chain(0, me, 1)
        z_after, z = chain(n_gx - 1, n_gx - 1 - me, -1)
    z_there = apply(op_out[1], z) + face_out[1].astype(F32)
    w_there = apply(op_out[0], w) + face_out[0].astype(F32)
    wave_rows(order[:2])
    w3, z3 = lift_weight * w, lift_weight * z

    position = lax.broadcasted_iota(jnp.int32, (x_points, columns), 0).astype(F32)
    left_prof = (x_points - position) / x_points
    right_prof = (position + 1.0) / x_points
    for i, (edge, y) in enumerate(((low_edge, 0), (high_edge, y_points - 1))):
        edge_out[i] = (
            edge + (left_prof * w3[y : y + 1, :] + right_prof * z3[y : y + 1, :])
        ).astype(BF16)

    def halo_copy(side, p):
        return pltpu.make_async_remote_copy(
            src_ref=edge_out.at[side],
            dst_ref=edge_in.at[1 - side],
            send_sem=halo_send.at[side],
            recv_sem=halo_recv.at[1 - side],
            device_id={"gy": p},
            device_id_type=MESH,
        )

    @pl.when(col > 0)
    def _():
        halo_copy(0, col - 1).start()

    @pl.when(col < n_gy - 1)
    def _():
        halo_copy(1, col + 1).start()

    inner_leaves(order[2:])
    wave_rows(order[2:])

    tip = 1.0 / x_points

    face = face_in[jnp.maximum(me - 1, 0)].astype(F32)
    there = face + lift_weight * (tip * w_before + z_there)
    grid[line(-1), :] = jnp.where(me > 0, there.astype(BF16).astype(F32), zeros)
    face = face_in[jnp.minimum(me + 1, n_gx - 1)].astype(F32)
    there = face + lift_weight * (w_there + tip * z_after)
    grid[line(x_points), :] = jnp.where(me < n_gx - 1, there.astype(BF16).astype(F32), zeros)

    def lift(x, carry):
        at = lax.convert_element_type(x, F32)
        u = grid[line(x), :] + (
            ((x_points - at) / x_points) * w3 + ((at + 1.0) / x_points) * z3
        )
        u = u.astype(BF16)
        upd_v[x] = u
        grid[line(x), :] = u.astype(F32)
        return carry

    lax.fori_loop(0, x_points, lift, 0, unroll=8)

    block = 4

    def finish(i, carry):
        x = i * block
        for low in range(0, y_points, q):
            part = slice(low, low + q)
            lines = [grid[line(x + j, low, q), :] for j in range(-1, block + 1)]
            for j in range(block):
                mid = lines[j + 1]
                near = (lines[j] + lines[j + 2]) + (
                    grid[line(x + j, low - 1, q), :] + grid[line(x + j, low + 1, q), :]
                )
                factor = wave_b[x + j, part, :] + kerr_b[x + j, part, :] * (mid * mid)
                value = near + (factor * mid - src_v[x + j, part, :].astype(F32))
                if low == 0:
                    rims[0, pl.ds(x + j, 1), :] = value[:1]
                if low + q == y_points:
                    rims[1, pl.ds(x + j, 1), :] = value[q - 1 :]
                res_v[x + j, part, :] = value.astype(BF16)
        return carry

    lax.fori_loop(0, x_points // block, finish, 0, unroll=2)

    @pl.when(col > 0)
    def _():
        halo_copy(1, col - 1).wait_recv()
        rims[0] = rims[0] + edge_in[0].astype(F32)

    @pl.when(col < n_gy - 1)
    def _():
        halo_copy(0, col + 1).wait_recv()
        rims[1] = rims[1] + edge_in[1].astype(F32)

    run(me + 1, n_gx, lambda p: face_copy(0, me, p).wait_send())
    run(0, me, lambda p: face_copy(1, me, p).wait_send())

    @pl.when(inner)
    def _():
        run(me + 1, n_gx, lambda p: op_copy(0, me, p).wait_send())
        run(0, me, lambda p: op_copy(1, me, p).wait_send())

    @pl.when(col > 0)
    def _():
        halo_copy(0, col - 1).wait_send()

    @pl.when(col < n_gy - 1)
    def _():
        halo_copy(1, col + 1).wait_send()


def store(pieces, upd_v, res_v, rims, updated, residual, sides, sems):
    x_points, y_points, columns = upd_v.shape
    q = sides.shape[2]
    rows = x_points // pieces
    inner = pl.ds(q, y_points - 2 * q)
    copies = []

    def send(src, dst):
        copies.append(pltpu.make_async_copy(src, dst, sems.at[len(copies)]))
        copies[-1].start()

    for i in range(pieces):
        span = pl.ds(i * rows, rows)
        send(upd_v.at[span], updated.at[span])
    for i in range(pieces):
        span = pl.ds(i * rows, rows)
        send(res_v.at[span, inner, :], residual.at[span, inner, :])
    row = lax.broadcasted_iota(jnp.int32, (q, columns), 0)
    for side, low, at in ((0, 0, 0), (1, y_points - q, q - 1)):
        for x in range(x_points):
            tile = res_v[x, low : low + q, :].astype(F32)
            full = jnp.broadcast_to(rims[side, x : x + 1, :], (q, columns))
            sides[side, x] = jnp.where(row == at, full, tile).astype(BF16)
        send(sides.at[side], residual.at[:, pl.ds(low, q), :])
    for c in copies:
        c.wait()


def per_device(n_gx, n_gy, source, field, kerr, wave, leaf_ops, transfer_ops):
    x_points, y_points, columns = source.shape
    leaves_x, leaves_y, leaf_pts, _ = leaf_ops.shape
    q = x_points // leaves_x
    grid_shape = (x_points, y_points, columns)
    dma = pltpu.SemaphoreType.DMA
    in_hbm = pl.BlockSpec(memory_space=pltpu.HBM)
    in_vmem = pl.BlockSpec(memory_space=pltpu.VMEM)
    operands = [
        pltpu.with_memory_space_constraint(a, pltpu.HBM)
        for a in (source, field, kerr, wave, leaf_ops, transfer_ops)
    ]
    results = pl.pallas_call(
        functools.partial(kernel, n_gx, n_gy),
        out_shape=[
            pltpu.VMEM(grid_shape, BF16),
            pltpu.VMEM(grid_shape, BF16),
            pltpu.VMEM((2, x_points, columns), F32),
        ],
        in_specs=[in_hbm] * 6,
        out_specs=[in_vmem] * 3,
        scratch_shapes=[
            pltpu.VMEM(grid_shape, BF16),
            pltpu.VMEM(grid_shape, BF16),
            pltpu.VMEM((x_points, y_points), F32),
            pltpu.VMEM((x_points, y_points), F32),
            pltpu.VMEM((y_points, y_points), F32),
            pltpu.VMEM(leaf_ops.shape, BF16),
            pltpu.VMEM((2, leaves_y, q, leaf_pts), BF16),
            pltpu.VMEM((leaves_x, leaves_y, leaf_pts, columns), BF16),
            pltpu.VMEM(((x_points + 2) * (y_points + 2 * PAD), columns), F32),
            pltpu.VMEM(grid_shape, F32),
            pltpu.VMEM(grid_shape, F32),
            pltpu.VMEM((2, y_points, columns), BF16),
            pltpu.VMEM((n_gx, y_points, columns), BF16),
            pltpu.VMEM((2, y_points // 2, 2 * y_points), BF16),
            pltpu.VMEM((n_gx, y_points // 2, 2 * y_points), BF16),
            pltpu.VMEM((2, x_points, columns), BF16),
            pltpu.VMEM((2, x_points, columns), BF16),
            dma((2, leaves_x)),
            dma((3,)),
            dma((leaves_x,)),
            dma((2,)),
            dma((n_gx,)),
            dma((n_gx,)),
            dma((n_gx,)),
            dma((n_gx,)),
            dma((2,)),
            dma((2,)),
        ],
        compiler_params=pltpu.CompilerParams(
            collective_id=0, has_side_effects=True, vmem_limit_bytes=40 * 1024 * 1024
        ),
        cost_estimate=pl.CostEstimate(
            flops=2 * leaf_ops.size * columns, bytes_accessed=6 << 20, transcendentals=0
        ),
        name="kerr_step",
    )(*operands)
    return pl.pallas_call(
        functools.partial(store, leaves_x),
        out_shape=[pltpu.HBM(grid_shape, BF16)] * 2,
        in_specs=[in_vmem] * 3,
        out_specs=[in_hbm] * 2,
        scratch_shapes=[
            pltpu.VMEM((2, x_points, q, columns), BF16),
            dma((2 * leaves_x + 2,)),
        ],
        compiler_params=pltpu.CompilerParams(vmem_limit_bytes=2 * 1024 * 1024),
        cost_estimate=pl.CostEstimate(flops=0, bytes_accessed=4 << 20, transcendentals=0),
        name="store_results",
    )(*results)


def solution(mesh):
    return jax.shard_map(
        functools.partial(per_device, mesh.shape["gx"], mesh.shape["gy"]),
        mesh=mesh,
        in_specs=(
            P(("grp", "gx"), "gy", None),
            P(("grp", "gx"), "gy", None),
            P(("grp", "gx"), "gy"),
            P(("grp", "gx"), "gy"),
            P("gx", "gy", None, None),
            P("gx", "gy", None),
        ),
        out_specs=(P(("grp", "gx"), "gy", None), P(("grp", "gx"), "gy", None)),
        check_vma=False,
    )
```

```python
import functools

import jax
import jax.numpy as jnp
from jax import lax
from jax.experimental import pallas as pl
from jax.experimental.pallas import tpu as pltpu
from jax.sharding import PartitionSpec as P

lift_weight = 0.3
MESH = pl.DeviceIdType.MESH
F32 = jnp.float32
BF16 = jnp.bfloat16
PAD = 8


def kernel(
    n_gx, n_gy,
    source, field, kerr, wave, leaf_ops, transfer_ops,
    upd_v, res_v, rims,
    src_v, fld_v, kerr_v, wave_v, map_v, ops_v, edge_ops, leaf_src, grid, kerr_b, wave_b,
    face_out, face_in, op_out, op_in, edge_out, edge_in,
    row_sems, small_sems, ops_sems, edge_sems,
    face_send, face_recv, op_send, op_recv, halo_send, halo_recv,
):
    x_points, y_points, columns = src_v.shape
    leaves_x, leaves_y, leaf_pts, _ = ops_v.shape
    q = x_points // leaves_x
    half = y_points // 2
    last = leaves_x - 1
    me = lax.axis_index("gx")
    col = lax.axis_index("gy")

    pitch = y_points + 2 * PAD

    def line(x, low=0, size=y_points):
        start = pl.multiple_of((1 + x) * pitch, 8) + PAD
        return pl.ds(start + low, size)

    def down(y):
        return pl.ds(pitch + PAD + y, x_points, stride=pitch)

    small = [
        pltpu.make_async_copy(kerr, kerr_v, small_sems.at[0]),
        pltpu.make_async_copy(wave, wave_v, small_sems.at[1]),
        pltpu.make_async_copy(transfer_ops.at[0], map_v, small_sems.at[2]),
    ]
    small[0].start()
    small[1].start()
    order = [0, last] + list(range(1, last))
    rows, edges, ops = {}, [], {}
    for a in order:
        span = pl.ds(a * q, q)
        rows[a] = (
            pltpu.make_async_copy(source.at[span], src_v.at[span], row_sems.at[0, a]),
            pltpu.make_async_copy(field.at[span], fld_v.at[span], row_sems.at[1, a]),
        )
    for i, (a, first) in enumerate(((0, 0), (last, leaf_pts - q))):
        edges.append(
            pltpu.make_async_copy(
                leaf_ops.at[a, :, pl.ds(first, q), :], edge_ops.at[i], edge_sems.at[i]
            )
        )
    for a in order:
        ops[a] = pltpu.make_async_copy(leaf_ops.at[a], ops_v.at[a], ops_sems.at[a])
    rows[0][0].start()
    rows[0][1].start()
    edges[0].start()

    barrier = pltpu.get_barrier_semaphore()

    def greet(p, carry):
        @pl.when(p != me)
        def _():
            pl.semaphore_signal(barrier, inc=1, device_id={"gx": p}, device_id_type=MESH)

        return carry

    @pl.when(col > 0)
    def _():
        pl.semaphore_signal(barrier, inc=1, device_id={"gy": col - 1}, device_id_type=MESH)

    @pl.when(col < n_gy - 1)
    def _():
        pl.semaphore_signal(barrier, inc=1, device_id={"gy": col + 1}, device_id_type=MESH)

    partners = (n_gx - 1) + jnp.where(col > 0, 1, 0) + jnp.where(col < n_gy - 1, 1, 0)

    lax.fori_loop(0, n_gx, greet, 0)

    for a in order[1:2]:
        rows[a][0].start()
        rows[a][1].start()
    edges[1].start()
    small[2].start()

    small[0].wait()
    small[1].wait()
    coeff = jnp.transpose(jnp.concatenate([kerr_v[...], wave_v[...] - 4.0], axis=0))
    for a in order[2:]:
        rows[a][0].start()
        rows[a][1].start()
    for a in order:
        ops[a].start()

    def face_copy(side, slot, p):
        return pltpu.make_async_remote_copy(
            src_ref=face_out.at[side],
            dst_ref=face_in.at[slot],
            send_sem=face_send.at[p],
            recv_sem=face_recv.at[slot],
            device_id={"gx": p},
            device_id_type=MESH,
        )

    def op_copy(side, slot, p):
        return pltpu.make_async_remote_copy(
            src_ref=op_out.at[side],
            dst_ref=op_in.at[slot],
            send_sem=op_send.at[p],
            recv_sem=op_recv.at[slot],
            device_id={"gx": p},
            device_id_type=MESH,
        )

    def run(low, high, body):
        def step(p, carry):
            body(p)
            return carry

        lax.fori_loop(low, high, step, 0)

    inner = jnp.logical_and(me > 0, me < n_gx - 1)
    def leaf_row(a):
        for i in range(q):
            x = a * q + i
            k = jnp.broadcast_to(coeff[:, x : x + 1], (y_points, columns))
            kerr_b[x] = k
            f = fld_v[x].astype(F32)
            s = (src_v[x].astype(F32) - k * f * f * f).astype(BF16)
            for b in range(leaves_y):
                leaf_src[a, b, i * q : (i + 1) * q, :] = s[b * q : (b + 1) * q]

    for i, a in enumerate((0, last)):
        if i == 0 or last > 0:
            rows[a][0].wait()
            rows[a][1].wait()
            leaf_row(a)
        edges[i].wait()
        for b in range(leaves_y):
            face_out[1 - i, b * q : (b + 1) * q, :] = jnp.dot(
                edge_ops[i, b], leaf_src[a, b], preferred_element_type=F32
            ).astype(BF16)
        if i == 0:
            pl.semaphore_wait(barrier, partners)
            run(0, me, lambda p: face_copy(1, me, p).start())
        else:
            run(me + 1, n_gx, lambda p: face_copy(0, me, p).start())

    small[2].wait()
    own = map_v[...]
    own_t = jnp.transpose(own)
    for i, m in enumerate((own, own_t)):
        op_out[i] = jnp.concatenate([m[:half], m[half:]], axis=1).astype(BF16)

    @pl.when(inner)
    def _():
        run(me + 1, n_gx, lambda p: op_copy(0, me, p).start())
        run(0, me, lambda p: op_copy(1, me, p).start())

    for a in order[2:]:
        rows[a][0].wait()
        rows[a][1].wait()
    for a in order:
        ops[a].wait()
    def solve(a, b):
        solved = jnp.dot(ops_v[a, b], leaf_src[a, b], preferred_element_type=F32)
        for i in range(q):
            grid[line(a * q + i, b * q, q), :] = solved[i * q : (i + 1) * q]

    for a in order:
        if a not in order[:2]:
            leaf_row(a)
        for b in sorted({0, leaves_y - 1}):
            solve(a, b)
    blank = jnp.zeros((x_points, columns), F32)
    grid[down(-1), :] = blank
    grid[down(y_points), :] = blank
    low_edge = grid[down(0), :]
    high_edge = grid[down(y_points - 1), :]

    def inner_leaves(part):
        for a in part:
            for b in range(1, leaves_y - 1):
                solve(a, b)

    def wave_rows(part):
        for a in part:
            for x in range(a * q, (a + 1) * q):
                wave_b[x] = jnp.broadcast_to(
                    coeff[:, x_points + x : x_points + x + 1], (y_points, columns)
                )

    inner_leaves(order[:2])

    def apply(packed, state):
        s = state.astype(BF16)
        z = jnp.zeros_like(s)
        wide = jnp.concatenate(
            [jnp.concatenate([s, z], axis=1), jnp.concatenate([z, s], axis=1)], axis=0
        )
        out = jnp.dot(packed, wide, preferred_element_type=F32)
        return jnp.concatenate([out[:, :columns], out[:, columns:]], axis=0)

    zeros = jnp.zeros((y_points, columns), F32)

    def arrived(s):
        face_copy(0, s, s).wait_recv()
        return face_in[s].astype(F32)

    def chain(begin, count, step):
        def first():
            return arrived(begin)

        state = lax.cond(count > 0, first, lambda: zeros)

        def hop(i, carry):
            _, now = carry
            s = begin + step * i
            op_copy(0, s, s).wait_recv()
            nxt = apply(op_in[s], now) + arrived(s)
            return now, nxt

        return lax.fori_loop(1, count, hop, (zeros, state))

    def straight():
        def wait(s):
            face_copy(0, s, s).wait_recv()

            @pl.when(jnp.logical_and(s > 0, s < n_gx - 1))
            def _():
                op_copy(0, s, s).wait_recv()

        run(0, me, wait)
        run(me + 1, n_gx, wait)
        states = []
        for steps, before in (
            (range(n_gx - 1), lambda s: s < me),
            (range(n_gx - 1, 0, -1), lambda s: s > me),
        ):
            prev, now = zeros, zeros
            for s in steps:
                nxt = face_in[s].astype(F32)
                if s != steps[0]:
                    nxt = nxt + apply(op_in[s], now)
                take = before(s)
                prev, now = jnp.where(take, now, prev), jnp.where(take, nxt, now)
            states += [prev, now]
        return states

    if n_gx <= 8:
        w_before, w, z_after, z = straight()
    else:
        w_before, w = chain(0, me, 1)
        z_after, z = chain(n_gx - 1, n_gx - 1 - me, -1)
    w3, z3 = lift_weight * w, lift_weight * z

    position = lax.broadcasted_iota(jnp.int32, (x_points, columns), 0).astype(F32)
    left_prof = (x_points - position) / x_points
    right_prof = (position + 1.0) / x_points
    for i, (edge, y) in enumerate(((low_edge, 0), (high_edge, y_points - 1))):
        edge_out[i] = (
            edge + (left_prof * w3[y : y + 1, :] + right_prof * z3[y : y + 1, :])
        ).astype(BF16)

    def halo_copy(side, p):
        return pltpu.make_async_remote_copy(
            src_ref=edge_out.at[side],
            dst_ref=edge_in.at[1 - side],
            send_sem=halo_send.at[side],
            recv_sem=halo_recv.at[1 - side],
            device_id={"gy": p},
            device_id_type=MESH,
        )

    @pl.when(col > 0)
    def _():
        halo_copy(0, col - 1).start()

    @pl.when(col < n_gy - 1)
    def _():
        halo_copy(1, col + 1).start()

    inner_leaves(order[2:])
    wave_rows(order)
    z_there = apply(op_out[1], z) + face_out[1].astype(F32)
    w_there = apply(op_out[0], w) + face_out[0].astype(F32)

    tip = 1.0 / x_points

    face = face_in[jnp.maximum(me - 1, 0)].astype(F32)
    there = face + lift_weight * (tip * w_before + z_there)
    grid[line(-1), :] = jnp.where(me > 0, there.astype(BF16).astype(F32), zeros)
    face = face_in[jnp.minimum(me + 1, n_gx - 1)].astype(F32)
    there = face + lift_weight * (w_there + tip * z_after)
    grid[line(x_points), :] = jnp.where(me < n_gx - 1, there.astype(BF16).astype(F32), zeros)

    def lift(x, carry):
        at = lax.convert_element_type(x, F32)
        u = grid[line(x), :] + (
            ((x_points - at) / x_points) * w3 + ((at + 1.0) / x_points) * z3
        )
        u = u.astype(BF16)
        upd_v[x] = u
        grid[line(x), :] = u.astype(F32)
        return carry

    lax.fori_loop(0, x_points, lift, 0, unroll=8)

    block = 4

    def finish(i, carry):
        x = i * block
        for low in range(0, y_points, q):
            part = slice(low, low + q)
            lines = [grid[line(x + j, low, q), :] for j in range(-1, block + 1)]
            for j in range(block):
                mid = lines[j + 1]
                near = (lines[j] + lines[j + 2]) + (
                    grid[line(x + j, low - 1, q), :] + grid[line(x + j, low + 1, q), :]
                )
                factor = wave_b[x + j, part, :] + kerr_b[x + j, part, :] * (mid * mid)
                value = near + (factor * mid - src_v[x + j, part, :].astype(F32))
                if low == 0:
                    rims[0, pl.ds(x + j, 1), :] = value[:1]
                if low + q == y_points:
                    rims[1, pl.ds(x + j, 1), :] = value[q - 1 :]
                res_v[x + j, part, :] = value.astype(BF16)
        return carry

    lax.fori_loop(0, x_points // block, finish, 0, unroll=2)

    @pl.when(col > 0)
    def _():
        halo_copy(1, col - 1).wait_recv()
        rims[0] = rims[0] + edge_in[0].astype(F32)

    @pl.when(col < n_gy - 1)
    def _():
        halo_copy(0, col + 1).wait_recv()
        rims[1] = rims[1] + edge_in[1].astype(F32)

    run(me + 1, n_gx, lambda p: face_copy(0, me, p).wait_send())
    run(0, me, lambda p: face_copy(1, me, p).wait_send())

    @pl.when(inner)
    def _():
        run(me + 1, n_gx, lambda p: op_copy(0, me, p).wait_send())
        run(0, me, lambda p: op_copy(1, me, p).wait_send())

    @pl.when(col > 0)
    def _():
        halo_copy(0, col - 1).wait_send()

    @pl.when(col < n_gy - 1)
    def _():
        halo_copy(1, col + 1).wait_send()


def store(pieces, upd_v, res_v, rims, updated, residual, sides, sems):
    x_points, y_points, columns = upd_v.shape
    q = sides.shape[2]
    rows = x_points // pieces
    inner = pl.ds(q, y_points - 2 * q)
    copies = []

    def send(src, dst):
        copies.append(pltpu.make_async_copy(src, dst, sems.at[len(copies)]))
        copies[-1].start()

    for i in range(pieces):
        span = pl.ds(i * rows, rows)
        send(upd_v.at[span], updated.at[span])
    for i in range(pieces):
        span = pl.ds(i * rows, rows)
        send(res_v.at[span, inner, :], residual.at[span, inner, :])
    row = lax.broadcasted_iota(jnp.int32, (q, columns), 0)
    for side, low, at in ((0, 0, 0), (1, y_points - q, q - 1)):
        for x in range(x_points):
            tile = res_v[x, low : low + q, :].astype(F32)
            full = jnp.broadcast_to(rims[side, x : x + 1, :], (q, columns))
            sides[side, x] = jnp.where(row == at, full, tile).astype(BF16)
        send(sides.at[side], residual.at[:, pl.ds(low, q), :])
    for c in copies:
        c.wait()


def per_device(n_gx, n_gy, source, field, kerr, wave, leaf_ops, transfer_ops):
    x_points, y_points, columns = source.shape
    leaves_x, leaves_y, leaf_pts, _ = leaf_ops.shape
    q = x_points // leaves_x
    grid_shape = (x_points, y_points, columns)
    dma = pltpu.SemaphoreType.DMA
    in_hbm = pl.BlockSpec(memory_space=pltpu.HBM)
    in_vmem = pl.BlockSpec(memory_space=pltpu.VMEM)
    operands = [
        pltpu.with_memory_space_constraint(a, pltpu.HBM)
        for a in (source, field, kerr, wave, leaf_ops, transfer_ops)
    ]
    results = pl.pallas_call(
        functools.partial(kernel, n_gx, n_gy),
        out_shape=[
            pltpu.VMEM(grid_shape, BF16),
            pltpu.VMEM(grid_shape, BF16),
            pltpu.VMEM((2, x_points, columns), F32),
        ],
        in_specs=[in_hbm] * 6,
        out_specs=[in_vmem] * 3,
        scratch_shapes=[
            pltpu.VMEM(grid_shape, BF16),
            pltpu.VMEM(grid_shape, BF16),
            pltpu.VMEM((x_points, y_points), F32),
            pltpu.VMEM((x_points, y_points), F32),
            pltpu.VMEM((y_points, y_points), F32),
            pltpu.VMEM(leaf_ops.shape, BF16),
            pltpu.VMEM((2, leaves_y, q, leaf_pts), BF16),
            pltpu.VMEM((leaves_x, leaves_y, leaf_pts, columns), BF16),
            pltpu.VMEM(((x_points + 2) * (y_points + 2 * PAD), columns), F32),
            pltpu.VMEM(grid_shape, F32),
            pltpu.VMEM(grid_shape, F32),
            pltpu.VMEM((2, y_points, columns), BF16),
            pltpu.VMEM((n_gx, y_points, columns), BF16),
            pltpu.VMEM((2, y_points // 2, 2 * y_points), BF16),
            pltpu.VMEM((n_gx, y_points // 2, 2 * y_points), BF16),
            pltpu.VMEM((2, x_points, columns), BF16),
            pltpu.VMEM((2, x_points, columns), BF16),
            dma((2, leaves_x)),
            dma((3,)),
            dma((leaves_x,)),
            dma((2,)),
            dma((n_gx,)),
            dma((n_gx,)),
            dma((n_gx,)),
            dma((n_gx,)),
            dma((2,)),
            dma((2,)),
        ],
        compiler_params=pltpu.CompilerParams(
            collective_id=0, has_side_effects=True, vmem_limit_bytes=40 * 1024 * 1024
        ),
        cost_estimate=pl.CostEstimate(
            flops=2 * leaf_ops.size * columns, bytes_accessed=6 << 20, transcendentals=0
        ),
        name="kerr_step",
    )(*operands)
    return pl.pallas_call(
        functools.partial(store, leaves_x),
        out_shape=[pltpu.HBM(grid_shape, BF16)] * 2,
        in_specs=[in_vmem] * 3,
        out_specs=[in_hbm] * 2,
        scratch_shapes=[
            pltpu.VMEM((2, x_points, q, columns), BF16),
            dma((2 * leaves_x + 2,)),
        ],
        compiler_params=pltpu.CompilerParams(vmem_limit_bytes=2 * 1024 * 1024),
        cost_estimate=pl.CostEstimate(flops=0, bytes_accessed=4 << 20, transcendentals=0),
        name="store_results",
    )(*results)


def solution(mesh):
    return jax.shard_map(
        functools.partial(per_device, mesh.shape["gx"], mesh.shape["gy"]),
        mesh=mesh,
        in_specs=(
            P(("grp", "gx"), "gy", None),
            P(("grp", "gx"), "gy", None),
            P(("grp", "gx"), "gy"),
            P(("grp", "gx"), "gy"),
            P("gx", "gy", None, None),
            P("gx", "gy", None),
        ),
        out_specs=(P(("grp", "gx"), "gy", None), P(("grp", "gx"), "gy", None)),
        check_vma=False,
    )
```

```python
import functools

import jax
import jax.numpy as jnp
from jax import lax
from jax.experimental import pallas as pl
from jax.experimental.pallas import tpu as pltpu
from jax.sharding import PartitionSpec as P

lift_weight = 0.3
MESH = pl.DeviceIdType.MESH
F32 = jnp.float32
BF16 = jnp.bfloat16
PAD = 8


def kernel(
    n_gx, n_gy,
    source, field, kerr, wave, leaf_ops, transfer_ops,
    upd_v, res_v, rims,
    src_v, fld_v, kerr_v, wave_v, map_v, ops_v, edge_ops, leaf_src, grid, kerr_b, wave_b,
    face_out, face_in, op_out, op_in, edge_out, edge_in, face_in_2, op_in_2,
    row_sems, small_sems, ops_sems, edge_sems,
    face_send, face_recv, op_send, op_recv, halo_send, halo_recv,
    face_send_2, face_recv_2, op_send_2, op_recv_2,
):
    x_points, y_points, columns = src_v.shape
    leaves_x, leaves_y, leaf_pts, _ = ops_v.shape
    q = x_points // leaves_x
    half = y_points // 2
    last = leaves_x - 1
    me = lax.axis_index("gx")
    col = lax.axis_index("gy")
    odd = lax.rem(col, 2)
    low_pair = jnp.logical_and(odd == 0, col > 0)
    high_pair = jnp.logical_and(odd == 1, col < n_gy - 1)
    has_pair = jnp.logical_or(low_pair, high_pair)
    pair = jnp.where(high_pair, col + 1, jnp.where(low_pair, col - 1, col))

    pitch = y_points + 2 * PAD

    def line(x, low=0, size=y_points):
        start = pl.multiple_of((1 + x) * pitch, 8) + PAD
        return pl.ds(start + low, size)

    def down(y):
        return pl.ds(pitch + PAD + y, x_points, stride=pitch)

    small = [
        pltpu.make_async_copy(kerr, kerr_v, small_sems.at[0]),
        pltpu.make_async_copy(wave, wave_v, small_sems.at[1]),
        pltpu.make_async_copy(transfer_ops.at[0], map_v, small_sems.at[2]),
    ]
    small[0].start()
    small[1].start()
    order = [0, last] + list(range(1, last))
    rows, edges, ops = {}, [], {}
    for a in order:
        span = pl.ds(a * q, q)
        rows[a] = (
            pltpu.make_async_copy(source.at[span], src_v.at[span], row_sems.at[0, a]),
            pltpu.make_async_copy(field.at[span], fld_v.at[span], row_sems.at[1, a]),
        )
    for i, (a, first) in enumerate(((0, 0), (last, leaf_pts - q))):
        edges.append(
            pltpu.make_async_copy(
                leaf_ops.at[a, :, pl.ds(first, q), :], edge_ops.at[i], edge_sems.at[i]
            )
        )
    for a in order:
        ops[a] = pltpu.make_async_copy(leaf_ops.at[a], ops_v.at[a], ops_sems.at[a])
    rows[0][0].start()
    rows[0][1].start()
    edges[0].start()

    barrier = pltpu.get_barrier_semaphore()

    def greet(p, carry):
        @pl.when(p != me)
        def _():
            pl.semaphore_signal(barrier, inc=1, device_id={"gx": p}, device_id_type=MESH)

            @pl.when(has_pair)
            def _():
                pl.semaphore_signal(
                    barrier, inc=1, device_id={"gx": p, "gy": pair}, device_id_type=MESH
                )

        return carry

    @pl.when(col > 0)
    def _():
        pl.semaphore_signal(barrier, inc=1, device_id={"gy": col - 1}, device_id_type=MESH)

    @pl.when(col < n_gy - 1)
    def _():
        pl.semaphore_signal(barrier, inc=1, device_id={"gy": col + 1}, device_id_type=MESH)

    partners = (n_gx - 1) + jnp.where(col > 0, 1, 0) + jnp.where(col < n_gy - 1, 1, 0)
    partners = partners + jnp.where(has_pair, n_gx - 1, 0)

    lax.fori_loop(0, n_gx, greet, 0)

    for a in order[1:2]:
        rows[a][0].start()
        rows[a][1].start()
    edges[1].start()
    small[2].start()

    small[0].wait()
    small[1].wait()
    coeff = jnp.transpose(jnp.concatenate([kerr_v[...], wave_v[...] - 4.0], axis=0))
    for a in order[2:]:
        rows[a][0].start()
        rows[a][1].start()
    for a in order:
        ops[a].start()

    def face_copy(side, slot, p, other=False):
        return pltpu.make_async_remote_copy(
            src_ref=face_out.at[side],
            dst_ref=(face_in_2 if other else face_in).at[slot],
            send_sem=(face_send_2 if other else face_send).at[p],
            recv_sem=(face_recv_2 if other else face_recv).at[slot],
            device_id={"gx": p, "gy": pair} if other else {"gx": p},
            device_id_type=MESH,
        )

    def op_copy(side, slot, p, other=False):
        return pltpu.make_async_remote_copy(
            src_ref=op_out.at[side],
            dst_ref=(op_in_2 if other else op_in).at[slot],
            send_sem=(op_send_2 if other else op_send).at[p],
            recv_sem=(op_recv_2 if other else op_recv).at[slot],
            device_id={"gx": p, "gy": pair} if other else {"gx": p},
            device_id_type=MESH,
        )

    def halo_copy(side, p):
        return pltpu.make_async_remote_copy(
            src_ref=edge_out.at[side],
            dst_ref=edge_in.at[1 - side],
            send_sem=halo_send.at[side],
            recv_sem=halo_recv.at[1 - side],
            device_id={"gy": p},
            device_id_type=MESH,
        )

    def run(low, high, body):
        def step(p, carry):
            body(p)
            return carry

        lax.fori_loop(low, high, step, 0)

    inner = jnp.logical_and(me > 0, me < n_gx - 1)
    low_end = jnp.where(has_pair, me, 0)
    high_end = jnp.where(has_pair, n_gx, me + 1)
    def leaf_row(a):
        for i in range(q):
            x = a * q + i
            k = jnp.broadcast_to(coeff[:, x : x + 1], (y_points, columns))
            kerr_b[x] = k
            f = fld_v[x].astype(F32)
            s = (src_v[x].astype(F32) - k * f * f * f).astype(BF16)
            for b in range(leaves_y):
                leaf_src[a, b, i * q : (i + 1) * q, :] = s[b * q : (b + 1) * q]

    for i, a in enumerate((0, last)):
        if i == 0 or last > 0:
            rows[a][0].wait()
            rows[a][1].wait()
            leaf_row(a)
        edges[i].wait()
        for b in range(leaves_y):
            face_out[1 - i, b * q : (b + 1) * q, :] = jnp.dot(
                edge_ops[i, b], leaf_src[a, b], preferred_element_type=F32
            ).astype(BF16)
        if i == 0:
            pl.semaphore_wait(barrier, partners)
            run(0, me, lambda p: face_copy(1, me, p).start())
            run(0, low_end, lambda p: face_copy(1, me, p, True).start())
        else:
            run(me + 1, n_gx, lambda p: face_copy(0, me, p).start())
            run(me + 1, high_end, lambda p: face_copy(0, me, p, True).start())

    small[2].wait()
    own = map_v[...]
    own_t = jnp.transpose(own)
    for i, m in enumerate((own, own_t)):
        op_out[i] = jnp.concatenate([m[:half], m[half:]], axis=1).astype(BF16)

    @pl.when(inner)
    def _():
        run(me + 1, n_gx, lambda p: op_copy(0, me, p).start())
        run(0, me, lambda p: op_copy(1, me, p).start())
        run(me + 1, high_end, lambda p: op_copy(0, me, p, True).start())
        run(0, low_end, lambda p: op_copy(1, me, p, True).start())

    for a in order[2:]:
        rows[a][0].wait()
        rows[a][1].wait()
    for a in order:
        ops[a].wait()
    def solve(a, b):
        solved = jnp.dot(ops_v[a, b], leaf_src[a, b], preferred_element_type=F32)
        for i in range(q):
            grid[line(a * q + i, b * q, q), :] = solved[i * q : (i + 1) * q]

    for a in order:
        if a not in order[:2]:
            leaf_row(a)
        for b in sorted({0, leaves_y - 1}):
            solve(a, b)
    blank = jnp.zeros((x_points, columns), F32)
    grid[down(-1), :] = blank
    grid[down(y_points), :] = blank
    low_edge = grid[down(0), :]
    high_edge = grid[down(y_points - 1), :]

    def inner_leaves(part):
        for a in part:
            for b in range(1, leaves_y - 1):
                solve(a, b)

    def wave_rows(part):
        for a in part:
            for x in range(a * q, (a + 1) * q):
                wave_b[x] = jnp.broadcast_to(
                    coeff[:, x_points + x : x_points + x + 1], (y_points, columns)
                )

    inner_leaves(order[:2])

    @pl.when(low_pair)
    def _():
        edge_out[0] = low_edge.astype(BF16)
        halo_copy(0, col - 1).start()

    @pl.when(high_pair)
    def _():
        edge_out[1] = high_edge.astype(BF16)
        halo_copy(1, col + 1).start()

    def apply(packed, state):
        s = state.astype(BF16)
        z = jnp.zeros_like(s)
        wide = jnp.concatenate(
            [jnp.concatenate([s, z], axis=1), jnp.concatenate([z, s], axis=1)], axis=0
        )
        out = jnp.dot(packed, wide, preferred_element_type=F32)
        return jnp.concatenate([out[:, :columns], out[:, columns:]], axis=0)

    zeros = jnp.zeros((y_points, columns), F32)

    def chain(begin, count, step, other):
        faces, ops_in = (face_in_2, op_in_2) if other else (face_in, op_in)

        def arrived(s):
            face_copy(0, s, s, other).wait_recv()
            return faces[s].astype(F32)

        state = lax.cond(count > 0, lambda: arrived(begin), lambda: zeros)

        def hop(i, carry):
            _, now = carry
            s = begin + step * i
            op_copy(0, s, s, other).wait_recv()
            return now, apply(ops_in[s], now) + arrived(s)

        return lax.fori_loop(1, count, hop, (zeros, state))

    def straight(other):
        faces, ops_in = (face_in_2, op_in_2) if other else (face_in, op_in)

        def wait(s):
            face_copy(0, s, s, other).wait_recv()

            @pl.when(jnp.logical_and(s > 0, s < n_gx - 1))
            def _():
                op_copy(0, s, s, other).wait_recv()

        run(0, low_end if other else me, wait)
        run(me + 1, high_end if other else n_gx, wait)
        states = []
        for steps, before in (
            (range(n_gx - 1), lambda s: s < me),
            (range(n_gx - 1, 0, -1), lambda s: s > me),
        ):
            prev, now = zeros, zeros
            for s in steps:
                nxt = faces[s].astype(F32)
                if s != steps[0]:
                    nxt = nxt + apply(ops_in[s], now)
                take = before(s)
                prev, now = jnp.where(take, now, prev), jnp.where(take, nxt, now)
            states += [prev, now]
        return states

    def chains(other):
        if n_gx <= 8:
            return straight(other)
        before, after = me, n_gx - 1 - me
        if other:
            before, after = jnp.where(has_pair, before, 0), jnp.where(has_pair, after, 0)
        return (*chain(0, before, 1, other), *chain(n_gx - 1, after, -1, other))

    w_before, w, z_after, z = chains(False)
    w3, z3 = lift_weight * w, lift_weight * z

    position = lax.broadcasted_iota(jnp.int32, (x_points, columns), 0).astype(F32)
    left_prof = (x_points - position) / x_points
    right_prof = (position + 1.0) / x_points

    def lifted(edge, w_side, z_side, y):
        return (
            edge + (left_prof * w_side[y : y + 1, :] + right_prof * z_side[y : y + 1, :])
        ).astype(BF16)

    @pl.when(odd == 1)
    def _():
        edge_out[0] = lifted(low_edge, w3, z3, 0)
        halo_copy(0, col - 1).start()

    @pl.when(jnp.logical_and(odd == 0, col < n_gy - 1))
    def _():
        edge_out[1] = lifted(high_edge, w3, z3, y_points - 1)
        halo_copy(1, col + 1).start()

    _, w_pair, _, z_pair = chains(True)
    w_pair, z_pair = lift_weight * w_pair, lift_weight * z_pair
    inner_leaves(order[2:])
    wave_rows(order)
    z_there = apply(op_out[1], z) + face_out[1].astype(F32)
    w_there = apply(op_out[0], w) + face_out[0].astype(F32)

    tip = 1.0 / x_points

    face = face_in[jnp.maximum(me - 1, 0)].astype(F32)
    there = face + lift_weight * (tip * w_before + z_there)
    grid[line(-1), :] = jnp.where(me > 0, there.astype(BF16).astype(F32), zeros)
    face = face_in[jnp.minimum(me + 1, n_gx - 1)].astype(F32)
    there = face + lift_weight * (w_there + tip * z_after)
    grid[line(x_points), :] = jnp.where(me < n_gx - 1, there.astype(BF16).astype(F32), zeros)

    def lift(x, carry):
        at = lax.convert_element_type(x, F32)
        u = grid[line(x), :] + (
            ((x_points - at) / x_points) * w3 + ((at + 1.0) / x_points) * z3
        )
        u = u.astype(BF16)
        upd_v[x] = u
        grid[line(x), :] = u.astype(F32)
        return carry

    lax.fori_loop(0, x_points, lift, 0, unroll=8)

    block = 4

    def finish(i, carry):
        x = i * block
        for low in range(0, y_points, q):
            part = slice(low, low + q)
            lines = [grid[line(x + j, low, q), :] for j in range(-1, block + 1)]
            for j in range(block):
                mid = lines[j + 1]
                near = (lines[j] + lines[j + 2]) + (
                    grid[line(x + j, low - 1, q), :] + grid[line(x + j, low + 1, q), :]
                )
                factor = wave_b[x + j, part, :] + kerr_b[x + j, part, :] * (mid * mid)
                value = near + (factor * mid - src_v[x + j, part, :].astype(F32))
                if low == 0:
                    rims[0, pl.ds(x + j, 1), :] = value[:1]
                if low + q == y_points:
                    rims[1, pl.ds(x + j, 1), :] = value[q - 1 :]
                res_v[x + j, part, :] = value.astype(BF16)
        return carry

    lax.fori_loop(0, x_points // block, finish, 0, unroll=2)

    @pl.when(col > 0)
    def _():
        halo_copy(1, col - 1).wait_recv()
        got = edge_in[0].astype(F32)
        full = lifted(got, w_pair, z_pair, y_points - 1).astype(F32)
        rims[0] = rims[0] + jnp.where(low_pair, full, got)

    @pl.when(col < n_gy - 1)
    def _():
        halo_copy(0, col + 1).wait_recv()
        got = edge_in[1].astype(F32)
        full = lifted(got, w_pair, z_pair, 0).astype(F32)
        rims[1] = rims[1] + jnp.where(high_pair, full, got)

    run(me + 1, n_gx, lambda p: face_copy(0, me, p).wait_send())
    run(0, me, lambda p: face_copy(1, me, p).wait_send())
    run(me + 1, high_end, lambda p: face_copy(0, me, p, True).wait_send())
    run(0, low_end, lambda p: face_copy(1, me, p, True).wait_send())

    @pl.when(inner)
    def _():
        run(me + 1, n_gx, lambda p: op_copy(0, me, p).wait_send())
        run(0, me, lambda p: op_copy(1, me, p).wait_send())
        run(me + 1, high_end, lambda p: op_copy(0, me, p, True).wait_send())
        run(0, low_end, lambda p: op_copy(1, me, p, True).wait_send())

    @pl.when(col > 0)
    def _():
        halo_copy(0, col - 1).wait_send()

    @pl.when(col < n_gy - 1)
    def _():
        halo_copy(1, col + 1).wait_send()


def store(pieces, upd_v, res_v, rims, updated, residual, sides, sems):
    x_points, y_points, columns = upd_v.shape
    q = sides.shape[2]
    rows = x_points // pieces
    inner = pl.ds(q, y_points - 2 * q)
    copies = []

    def send(src, dst):
        copies.append(pltpu.make_async_copy(src, dst, sems.at[len(copies)]))
        copies[-1].start()

    for i in range(pieces):
        span = pl.ds(i * rows, rows)
        send(upd_v.at[span], updated.at[span])
    for i in range(pieces):
        span = pl.ds(i * rows, rows)
        send(res_v.at[span, inner, :], residual.at[span, inner, :])
    row = lax.broadcasted_iota(jnp.int32, (q, columns), 0)
    for side, low, at in ((0, 0, 0), (1, y_points - q, q - 1)):
        for x in range(x_points):
            tile = res_v[x, low : low + q, :].astype(F32)
            full = jnp.broadcast_to(rims[side, x : x + 1, :], (q, columns))
            sides[side, x] = jnp.where(row == at, full, tile).astype(BF16)
        send(sides.at[side], residual.at[:, pl.ds(low, q), :])
    for c in copies:
        c.wait()


def per_device(n_gx, n_gy, source, field, kerr, wave, leaf_ops, transfer_ops):
    x_points, y_points, columns = source.shape
    leaves_x, leaves_y, leaf_pts, _ = leaf_ops.shape
    q = x_points // leaves_x
    grid_shape = (x_points, y_points, columns)
    dma = pltpu.SemaphoreType.DMA
    in_hbm = pl.BlockSpec(memory_space=pltpu.HBM)
    in_vmem = pl.BlockSpec(memory_space=pltpu.VMEM)
    operands = [
        pltpu.with_memory_space_constraint(a, pltpu.HBM)
        for a in (source, field, kerr, wave, leaf_ops, transfer_ops)
    ]
    results = pl.pallas_call(
        functools.partial(kernel, n_gx, n_gy),
        out_shape=[
            pltpu.VMEM(grid_shape, BF16),
            pltpu.VMEM(grid_shape, BF16),
            pltpu.VMEM((2, x_points, columns), F32),
        ],
        in_specs=[in_hbm] * 6,
        out_specs=[in_vmem] * 3,
        scratch_shapes=[
            pltpu.VMEM(grid_shape, BF16),
            pltpu.VMEM(grid_shape, BF16),
            pltpu.VMEM((x_points, y_points), F32),
            pltpu.VMEM((x_points, y_points), F32),
            pltpu.VMEM((y_points, y_points), F32),
            pltpu.VMEM(leaf_ops.shape, BF16),
            pltpu.VMEM((2, leaves_y, q, leaf_pts), BF16),
            pltpu.VMEM((leaves_x, leaves_y, leaf_pts, columns), BF16),
            pltpu.VMEM(((x_points + 2) * (y_points + 2 * PAD), columns), F32),
            pltpu.VMEM(grid_shape, F32),
            pltpu.VMEM(grid_shape, F32),
            pltpu.VMEM((2, y_points, columns), BF16),
            pltpu.VMEM((n_gx, y_points, columns), BF16),
            pltpu.VMEM((2, y_points // 2, 2 * y_points), BF16),
            pltpu.VMEM((n_gx, y_points // 2, 2 * y_points), BF16),
            pltpu.VMEM((2, x_points, columns), BF16),
            pltpu.VMEM((2, x_points, columns), BF16),
            pltpu.VMEM((n_gx, y_points, columns), BF16),
            pltpu.VMEM((n_gx, y_points // 2, 2 * y_points), BF16),
            dma((2, leaves_x)),
            dma((3,)),
            dma((leaves_x,)),
            dma((2,)),
            dma((n_gx,)),
            dma((n_gx,)),
            dma((n_gx,)),
            dma((n_gx,)),
            dma((2,)),
            dma((2,)),
            *[dma((n_gx,))] * 4,
        ],
        compiler_params=pltpu.CompilerParams(
            collective_id=0, has_side_effects=True, vmem_limit_bytes=40 * 1024 * 1024
        ),
        cost_estimate=pl.CostEstimate(
            flops=2 * leaf_ops.size * columns, bytes_accessed=6 << 20, transcendentals=0
        ),
        name="kerr_step",
    )(*operands)
    return pl.pallas_call(
        functools.partial(store, leaves_x),
        out_shape=[pltpu.HBM(grid_shape, BF16)] * 2,
        in_specs=[in_vmem] * 3,
        out_specs=[in_hbm] * 2,
        scratch_shapes=[
            pltpu.VMEM((2, x_points, q, columns), BF16),
            dma((2 * leaves_x + 2,)),
        ],
        compiler_params=pltpu.CompilerParams(vmem_limit_bytes=2 * 1024 * 1024),
        cost_estimate=pl.CostEstimate(flops=0, bytes_accessed=4 << 20, transcendentals=0),
        name="store_results",
    )(*results)


def solution(mesh):
    return jax.shard_map(
        functools.partial(per_device, mesh.shape["gx"], mesh.shape["gy"]),
        mesh=mesh,
        in_specs=(
            P(("grp", "gx"), "gy", None),
            P(("grp", "gx"), "gy", None),
            P(("grp", "gx"), "gy"),
            P(("grp", "gx"), "gy"),
            P("gx", "gy", None, None),
            P("gx", "gy", None),
        ),
        out_specs=(P(("grp", "gx"), "gy", None), P(("grp", "gx"), "gy", None)),
        check_vma=False,
    )
```

```python
import functools

import jax
import jax.numpy as jnp
from jax import lax
from jax.experimental import pallas as pl
from jax.experimental.pallas import tpu as pltpu
from jax.sharding import PartitionSpec as P

lift_weight = 0.3
MESH = pl.DeviceIdType.MESH
F32 = jnp.float32
BF16 = jnp.bfloat16
PAD = 8


def kernel(
    n_gx, n_gy,
    source, field, kerr, wave, leaf_ops, transfer_ops,
    upd_v, res_v, rims,
    src_v, fld_v, kerr_v, wave_v, map_v, ops_v, edge_ops, leaf_src, grid, kerr_b, wave_b,
    face_out, face_in, op_out, op_in, edge_out, edge_in,
    row_sems, small_sems, ops_sems, edge_sems,
    face_send, face_recv, op_send, op_recv, halo_send, halo_recv,
):
    x_points, y_points, columns = src_v.shape
    leaves_x, leaves_y, leaf_pts, _ = ops_v.shape
    q = x_points // leaves_x
    half = y_points // 2
    last = leaves_x - 1
    me = lax.axis_index("gx")
    col = lax.axis_index("gy")

    pitch = y_points + 2 * PAD

    def line(x, low=0, size=y_points):
        start = pl.multiple_of((1 + x) * pitch, 8) + PAD
        return pl.ds(start + low, size)

    def down(y):
        return pl.ds(pitch + PAD + y, x_points, stride=pitch)

    small = [
        pltpu.make_async_copy(kerr, kerr_v, small_sems.at[0]),
        pltpu.make_async_copy(wave, wave_v, small_sems.at[1]),
        pltpu.make_async_copy(transfer_ops.at[0], map_v, small_sems.at[2]),
    ]
    small[0].start()
    small[1].start()
    order = [0, last] + list(range(1, last))
    rows, edges, ops = {}, [], {}
    for a in order:
        span = pl.ds(a * q, q)
        rows[a] = (
            pltpu.make_async_copy(source.at[span], src_v.at[span], row_sems.at[0, a]),
            pltpu.make_async_copy(field.at[span], fld_v.at[span], row_sems.at[1, a]),
        )
    for i, (a, first) in enumerate(((0, 0), (last, leaf_pts - q))):
        edges.append(
            pltpu.make_async_copy(
                leaf_ops.at[a, :, pl.ds(first, q), :], edge_ops.at[i], edge_sems.at[i]
            )
        )
    for a in order:
        ops[a] = pltpu.make_async_copy(leaf_ops.at[a], ops_v.at[a], ops_sems.at[a])
    rows[0][0].start()
    rows[0][1].start()
    edges[0].start()

    barrier = pltpu.get_barrier_semaphore()

    def greet(p, carry):
        @pl.when(p != me)
        def _():
            pl.semaphore_signal(barrier, inc=1, device_id={"gx": p}, device_id_type=MESH)

        return carry

    @pl.when(col > 0)
    def _():
        pl.semaphore_signal(barrier, inc=1, device_id={"gy": col - 1}, device_id_type=MESH)

    @pl.when(col < n_gy - 1)
    def _():
        pl.semaphore_signal(barrier, inc=1, device_id={"gy": col + 1}, device_id_type=MESH)

    partners = (n_gx - 1) + jnp.where(col > 0, 1, 0) + jnp.where(col < n_gy - 1, 1, 0)

    lax.fori_loop(0, n_gx, greet, 0)

    for a in order[1:2]:
        rows[a][0].start()
        rows[a][1].start()
    edges[1].start()
    small[2].start()

    small[0].wait()
    small[1].wait()
    coeff = jnp.transpose(jnp.concatenate([kerr_v[...], wave_v[...] - 4.0], axis=0))
    for a in order[2:]:
        rows[a][0].start()
        rows[a][1].start()
    for a in order:
        ops[a].start()

    def face_copy(side, slot, p):
        return pltpu.make_async_remote_copy(
            src_ref=face_out.at[side],
            dst_ref=face_in.at[slot],
            send_sem=face_send.at[p],
            recv_sem=face_recv.at[slot],
            device_id={"gx": p},
            device_id_type=MESH,
        )

    def op_copy(side, slot, p):
        return pltpu.make_async_remote_copy(
            src_ref=op_out.at[side],
            dst_ref=op_in.at[slot],
            send_sem=op_send.at[p],
            recv_sem=op_recv.at[slot],
            device_id={"gx": p},
            device_id_type=MESH,
        )

    def run(low, high, body):
        def step(p, carry):
            body(p)
            return carry

        lax.fori_loop(low, high, step, 0)

    inner = jnp.logical_and(me > 0, me < n_gx - 1)
    def leaf_row(a):
        for i in range(q):
            x = a * q + i
            k = jnp.broadcast_to(coeff[:, x : x + 1], (y_points, columns))
            kerr_b[x] = k
            f = fld_v[x].astype(F32)
            s = (src_v[x].astype(F32) - k * f * f * f).astype(BF16)
            for b in range(leaves_y):
                leaf_src[a, b, i * q : (i + 1) * q, :] = s[b * q : (b + 1) * q]

    def pack():
        small[2].wait()
        own = map_v[...]
        for i, m in enumerate((own, jnp.transpose(own))):
            op_out[i] = jnp.concatenate([m[:half], m[half:]], axis=1).astype(BF16)

    for i, a in enumerate((0, last)):
        if i == 0 or last > 0:
            rows[a][0].wait()
            rows[a][1].wait()
            leaf_row(a)
        edges[i].wait()
        for b in range(leaves_y):
            face_out[1 - i, b * q : (b + 1) * q, :] = jnp.dot(
                edge_ops[i, b], leaf_src[a, b], preferred_element_type=F32
            ).astype(BF16)
        if i == 0:
            pl.when(inner)(pack)
            pl.semaphore_wait(barrier, partners)
            run(0, me, lambda p: face_copy(1, me, p).start())

            @pl.when(inner)
            def _():
                run(0, me, lambda p: op_copy(1, me, p).start())
                run(me + 1, n_gx, lambda p: op_copy(0, me, p).start())

        else:
            run(me + 1, n_gx, lambda p: face_copy(0, me, p).start())

    @pl.when(jnp.logical_not(inner))
    def _():
        pack()

    for a in order[2:]:
        rows[a][0].wait()
        rows[a][1].wait()
    for a in order:
        ops[a].wait()
    def solve(a, b):
        solved = jnp.dot(ops_v[a, b], leaf_src[a, b], preferred_element_type=F32)
        for i in range(q):
            grid[line(a * q + i, b * q, q), :] = solved[i * q : (i + 1) * q]

    for a in order:
        if a not in order[:2]:
            leaf_row(a)
        for b in sorted({0, leaves_y - 1}):
            solve(a, b)
    blank = jnp.zeros((x_points, columns), F32)
    grid[down(-1), :] = blank
    grid[down(y_points), :] = blank
    low_edge = grid[down(0), :]
    high_edge = grid[down(y_points - 1), :]

    def inner_leaves(part):
        for a in part:
            for b in range(1, leaves_y - 1):
                solve(a, b)

    def wave_rows(part):
        for a in part:
            for x in range(a * q, (a + 1) * q):
                wave_b[x] = jnp.broadcast_to(
                    coeff[:, x_points + x : x_points + x + 1], (y_points, columns)
                )

    inner_leaves(order[:2])

    def apply(packed, state):
        s = state.astype(BF16)
        z = jnp.zeros_like(s)
        wide = jnp.concatenate(
            [jnp.concatenate([s, z], axis=1), jnp.concatenate([z, s], axis=1)], axis=0
        )
        out = jnp.dot(packed, wide, preferred_element_type=F32)
        return jnp.concatenate([out[:, :columns], out[:, columns:]], axis=0)

    zeros = jnp.zeros((y_points, columns), F32)

    def arrived(s):
        face_copy(0, s, s).wait_recv()
        return face_in[s].astype(F32)

    def chain(begin, count, step):
        def first():
            return arrived(begin)

        state = lax.cond(count > 0, first, lambda: zeros)

        def hop(i, carry):
            _, now = carry
            s = begin + step * i
            op_copy(0, s, s).wait_recv()
            nxt = apply(op_in[s], now) + arrived(s)
            return now, nxt

        return lax.fori_loop(1, count, hop, (zeros, state))

    def straight():
        def wait(s):
            face_copy(0, s, s).wait_recv()

            @pl.when(jnp.logical_and(s > 0, s < n_gx - 1))
            def _():
                op_copy(0, s, s).wait_recv()

        run(0, me, wait)
        run(me + 1, n_gx, wait)
        states = []
        for steps, before in (
            (range(n_gx - 1), lambda s: s < me),
            (range(n_gx - 1, 0, -1), lambda s: s > me),
        ):
            prev, now = zeros, zeros
            for s in steps:
                nxt = face_in[s].astype(F32)
                if s != steps[0]:
                    nxt = nxt + apply(op_in[s], now)
                take = before(s)
                prev, now = jnp.where(take, now, prev), jnp.where(take, nxt, now)
            states += [prev, now]
        return states

    if n_gx <= 8:
        w_before, w, z_after, z = straight()
    else:
        w_before, w = chain(0, me, 1)
        z_after, z = chain(n_gx - 1, n_gx - 1 - me, -1)
    w3, z3 = lift_weight * w, lift_weight * z

    position = lax.broadcasted_iota(jnp.int32, (x_points, columns), 0).astype(F32)
    left_prof = (x_points - position) / x_points
    right_prof = (position + 1.0) / x_points
    for i, (edge, y) in enumerate(((low_edge, 0), (high_edge, y_points - 1))):
        edge_out[i] = (
            edge + (left_prof * w3[y : y + 1, :] + right_prof * z3[y : y + 1, :])
        ).astype(BF16)

    def halo_copy(side, p):
        return pltpu.make_async_remote_copy(
            src_ref=edge_out.at[side],
            dst_ref=edge_in.at[1 - side],
            send_sem=halo_send.at[side],
            recv_sem=halo_recv.at[1 - side],
            device_id={"gy": p},
            device_id_type=MESH,
        )

    @pl.when(col > 0)
    def _():
        halo_copy(0, col - 1).start()

    @pl.when(col < n_gy - 1)
    def _():
        halo_copy(1, col + 1).start()

    inner_leaves(order[2:])
    wave_rows(order)
    z_there = apply(op_out[1], z) + face_out[1].astype(F32)
    w_there = apply(op_out[0], w) + face_out[0].astype(F32)

    tip = 1.0 / x_points

    face = face_in[jnp.maximum(me - 1, 0)].astype(F32)
    there = face + lift_weight * (tip * w_before + z_there)
    grid[line(-1), :] = jnp.where(me > 0, there.astype(BF16).astype(F32), zeros)
    face = face_in[jnp.minimum(me + 1, n_gx - 1)].astype(F32)
    there = face + lift_weight * (w_there + tip * z_after)
    grid[line(x_points), :] = jnp.where(me < n_gx - 1, there.astype(BF16).astype(F32), zeros)

    def lift(x, carry):
        at = lax.convert_element_type(x, F32)
        u = grid[line(x), :] + (
            ((x_points - at) / x_points) * w3 + ((at + 1.0) / x_points) * z3
        )
        u = u.astype(BF16)
        upd_v[x] = u
        grid[line(x), :] = u.astype(F32)
        return carry

    lax.fori_loop(0, x_points, lift, 0, unroll=8)

    block = 4

    def finish(i, carry):
        x = i * block
        for low in range(0, y_points, q):
            part = slice(low, low + q)
            lines = [grid[line(x + j, low, q), :] for j in range(-1, block + 1)]
            for j in range(block):
                mid = lines[j + 1]
                near = (lines[j] + lines[j + 2]) + (
                    grid[line(x + j, low - 1, q), :] + grid[line(x + j, low + 1, q), :]
                )
                factor = wave_b[x + j, part, :] + kerr_b[x + j, part, :] * (mid * mid)
                value = near + (factor * mid - src_v[x + j, part, :].astype(F32))
                if low == 0:
                    rims[0, pl.ds(x + j, 1), :] = value[:1]
                if low + q == y_points:
                    rims[1, pl.ds(x + j, 1), :] = value[q - 1 :]
                res_v[x + j, part, :] = value.astype(BF16)
        return carry

    lax.fori_loop(0, x_points // block, finish, 0, unroll=2)

    @pl.when(col > 0)
    def _():
        halo_copy(1, col - 1).wait_recv()
        rims[0] = rims[0] + edge_in[0].astype(F32)

    @pl.when(col < n_gy - 1)
    def _():
        halo_copy(0, col + 1).wait_recv()
        rims[1] = rims[1] + edge_in[1].astype(F32)

    run(me + 1, n_gx, lambda p: face_copy(0, me, p).wait_send())
    run(0, me, lambda p: face_copy(1, me, p).wait_send())

    @pl.when(inner)
    def _():
        run(me + 1, n_gx, lambda p: op_copy(0, me, p).wait_send())
        run(0, me, lambda p: op_copy(1, me, p).wait_send())

    @pl.when(col > 0)
    def _():
        halo_copy(0, col - 1).wait_send()

    @pl.when(col < n_gy - 1)
    def _():
        halo_copy(1, col + 1).wait_send()


def store(pieces, upd_v, res_v, rims, updated, residual, sides, sems):
    x_points, y_points, columns = upd_v.shape
    q = sides.shape[2]
    rows = x_points // pieces
    inner = pl.ds(q, y_points - 2 * q)
    copies = []

    def send(src, dst):
        copies.append(pltpu.make_async_copy(src, dst, sems.at[len(copies)]))
        copies[-1].start()

    for i in range(pieces):
        span = pl.ds(i * rows, rows)
        send(upd_v.at[span], updated.at[span])
    for i in range(pieces):
        span = pl.ds(i * rows, rows)
        send(res_v.at[span, inner, :], residual.at[span, inner, :])
    row = lax.broadcasted_iota(jnp.int32, (q, columns), 0)
    for side, low, at in ((0, 0, 0), (1, y_points - q, q - 1)):
        for x in range(x_points):
            tile = res_v[x, low : low + q, :].astype(F32)
            full = jnp.broadcast_to(rims[side, x : x + 1, :], (q, columns))
            sides[side, x] = jnp.where(row == at, full, tile).astype(BF16)
        send(sides.at[side], residual.at[:, pl.ds(low, q), :])
    for c in copies:
        c.wait()


def per_device(n_gx, n_gy, source, field, kerr, wave, leaf_ops, transfer_ops):
    x_points, y_points, columns = source.shape
    leaves_x, leaves_y, leaf_pts, _ = leaf_ops.shape
    q = x_points // leaves_x
    grid_shape = (x_points, y_points, columns)
    dma = pltpu.SemaphoreType.DMA
    in_hbm = pl.BlockSpec(memory_space=pltpu.HBM)
    in_vmem = pl.BlockSpec(memory_space=pltpu.VMEM)
    operands = [
        pltpu.with_memory_space_constraint(a, pltpu.HBM)
        for a in (source, field, kerr, wave, leaf_ops, transfer_ops)
    ]
    results = pl.pallas_call(
        functools.partial(kernel, n_gx, n_gy),
        out_shape=[
            pltpu.VMEM(grid_shape, BF16),
            pltpu.VMEM(grid_shape, BF16),
            pltpu.VMEM((2, x_points, columns), F32),
        ],
        in_specs=[in_hbm] * 6,
        out_specs=[in_vmem] * 3,
        scratch_shapes=[
            pltpu.VMEM(grid_shape, BF16),
            pltpu.VMEM(grid_shape, BF16),
            pltpu.VMEM((x_points, y_points), F32),
            pltpu.VMEM((x_points, y_points), F32),
            pltpu.VMEM((y_points, y_points), F32),
            pltpu.VMEM(leaf_ops.shape, BF16),
            pltpu.VMEM((2, leaves_y, q, leaf_pts), BF16),
            pltpu.VMEM((leaves_x, leaves_y, leaf_pts, columns), BF16),
            pltpu.VMEM(((x_points + 2) * (y_points + 2 * PAD), columns), F32),
            pltpu.VMEM(grid_shape, F32),
            pltpu.VMEM(grid_shape, F32),
            pltpu.VMEM((2, y_points, columns), BF16),
            pltpu.VMEM((n_gx, y_points, columns), BF16),
            pltpu.VMEM((2, y_points // 2, 2 * y_points), BF16),
            pltpu.VMEM((n_gx, y_points // 2, 2 * y_points), BF16),
            pltpu.VMEM((2, x_points, columns), BF16),
            pltpu.VMEM((2, x_points, columns), BF16),
            dma((2, leaves_x)),
            dma((3,)),
            dma((leaves_x,)),
            dma((2,)),
            dma((n_gx,)),
            dma((n_gx,)),
            dma((n_gx,)),
            dma((n_gx,)),
            dma((2,)),
            dma((2,)),
        ],
        compiler_params=pltpu.CompilerParams(
            collective_id=0, has_side_effects=True, vmem_limit_bytes=40 * 1024 * 1024
        ),
        cost_estimate=pl.CostEstimate(
            flops=2 * leaf_ops.size * columns, bytes_accessed=6 << 20, transcendentals=0
        ),
        name="kerr_step",
    )(*operands)
    return pl.pallas_call(
        functools.partial(store, leaves_x),
        out_shape=[pltpu.HBM(grid_shape, BF16)] * 2,
        in_specs=[in_vmem] * 3,
        out_specs=[in_hbm] * 2,
        scratch_shapes=[
            pltpu.VMEM((2, x_points, q, columns), BF16),
            dma((2 * leaves_x + 2,)),
        ],
        compiler_params=pltpu.CompilerParams(vmem_limit_bytes=2 * 1024 * 1024),
        cost_estimate=pl.CostEstimate(flops=0, bytes_accessed=4 << 20, transcendentals=0),
        name="store_results",
    )(*results)


def solution(mesh):
    return jax.shard_map(
        functools.partial(per_device, mesh.shape["gx"], mesh.shape["gy"]),
        mesh=mesh,
        in_specs=(
            P(("grp", "gx"), "gy", None),
            P(("grp", "gx"), "gy", None),
            P(("grp", "gx"), "gy"),
            P(("grp", "gx"), "gy"),
            P("gx", "gy", None, None),
            P("gx", "gy", None),
        ),
        out_specs=(P(("grp", "gx"), "gy", None), P(("grp", "gx"), "gy", None)),
        check_vma=False,
    )
```
